256 devices in a mesh: row: 16 (over y, z_lo, core), col: 4 (over x), chan: 4 (over z_hi).
Axes of the slice: x: 4, y: 4, z: 8 (z_hi: 4, z_lo: 2; z = z_hi * 2 + z_lo), core: 2. Of those that a mesh axis runs over, the one named last changes fastest.
Arguments:
- pair: bfloat16 [128, 512, 512], P('chan', 'row', 'col'), may hold values from -6 to 6
- token_valid: int32 [512], replicated, may hold values from 0 to 1, as said below
- ln_gain: float32 [128], replicated, may hold values from 0.5 to 1.5
- ln_bias: float32 [128], replicated, may hold values from -3 to 3
- w_agate: bfloat16 [128, 128], P(None, 'chan'), may hold values from -0.5 to 0.5
- w_aproj: bfloat16 [128, 128], P(None, 'chan'), may hold values from -0.5 to 0.5
- w_bgate: bfloat16 [128, 128], P(None, 'chan'), may hold values from -0.5 to 0.5
- w_bproj: bfloat16 [128, 128], P(None, 'chan'), may hold values from -0.5 to 0.5
- w_gate: bfloat16 [128, 128], P(None, 'chan'), may hold values from -0.5 to 0.5
- out_gain: float32 [128], P('chan'), may hold values from 0.5 to 1.5
- out_bias: float32 [128], P('chan'), may hold values from -3 to 3
- w_out: bfloat16 [128, 128], replicated, may hold values from -0.5 to 0.5
Outputs:
- update: bfloat16 [128, 512, 512], P('chan', 'row', 'col')
The draws below stay inside these ranges and needn't reach their ends.
Inputs may be any that keep to these rules, and one draw needn't show every extreme that they name: token_valid is 1 for the first tokens of the complex and 0 for the padding after them; at least 256 tokens are real and the last token is padding.
All inputs are finite; a program needn't handle non-finite values.
Results may differ from the reference program's by a relative error of at most 0.015.
Values may be sent and summed in bfloat16 or wider, within the bound.
A program may use at most 64 MiB of HBM per device.

```python
import jax
import jax.numpy as jnp
from jax import lax

C = 128
N = 512


def draw_token_valid(key, part):
    key = jax.random.fold_in(key, 7)
    real_count = jax.random.randint(key, (), N // 2, N)
    return (jnp.arange(N) < real_count).astype(jnp.int32)


def levels(rng, shape, pieces, low, high):
    loudness, own = 1.0, jax.random.fold_in(rng, 6)
    for axis_at, shards_of in pieces:
        heights = jnp.exp(jax.random.uniform(jax.random.fold_in(own, axis_at), (shards_of,), jnp.float32, low / len(pieces), high / len(pieces)))
        loudness = loudness * jnp.repeat(heights, shape[axis_at] // shards_of).reshape([-1 if axis == axis_at else 1 for axis in range(len(shape))])
    return loudness


def scatter_about(rng, dims, scale, limit, cuts=(), dtype=jnp.bfloat16):
    level = levels(rng, dims, cuts, -0.22, 0.18) if cuts else 1.0
    result = jax.random.normal(rng, dims, jnp.float32) * scale * level
    return jnp.minimum(jnp.maximum(result, -limit), limit).astype(dtype)


def setup_inputs(seed: int = 0) -> dict:
    key_list = jax.random.split(jax.random.key(seed), 13)
    pair = scatter_about(key_list[0], (C, N, N), 1.0, 6.0, ((0, 4), (1, 16), (2, 4)))
    token_valid = draw_token_valid(jax.random.fold_in(key_list[12], 71), 0)
    ln_gain = jnp.clip(1.0 + 0.1 * jax.random.normal(key_list[2], (C,), jnp.float32), 0.5, 1.5)
    ln_bias = scatter_about(key_list[3], (C,), 0.5, 3.0, (), jnp.float32)
    w_agate = scatter_about(key_list[4], (C, C), C ** -0.5, 0.5, ((1, 4),))
    w_aproj = scatter_about(key_list[5], (C, C), C ** -0.5, 0.5, ((1, 4),))
    w_bgate = scatter_about(key_list[6], (C, C), C ** -0.5, 0.5, ((1, 4),))
    w_bproj = scatter_about(key_list[7], (C, C), C ** -0.5, 0.5, ((1, 4),))
    w_gate = scatter_about(key_list[8], (C, C), C ** -0.5, 0.5, ((1, 4),))
    out_gain = jnp.clip(1.0 + 0.1 * jax.random.normal(key_list[9], (C,), jnp.float32), 0.5, 1.5)
    out_bias = scatter_about(key_list[10], (C,), 0.5, 3.0, ((0, 4),), jnp.float32)
    w_out = scatter_about(key_list[11], (C, C), C ** -0.5, 0.5)
    return {"pair": pair, "token_valid": token_valid, "ln_gain": ln_gain, "ln_bias": ln_bias, "w_agate": w_agate, "w_aproj": w_aproj, "w_bgate": w_bgate, "w_bproj": w_bproj, "w_gate": w_gate, "out_gain": out_gain, "out_bias": out_bias, "w_out": w_out}


EPSILON = 1e-05

def layer_norm(values, gain, shift):
    centre = lax.optimization_barrier(jnp.mean(values, axis=0, keepdims=True))
    spread_sq = lax.optimization_barrier(jnp.mean(jnp.square(values - centre), axis=0, keepdims=True))
    return (values - centre) * lax.rsqrt(spread_sq + EPSILON) * gain[:, None, None] + shift[:, None, None]

def reference(pair, token_valid, ln_gain, ln_bias, w_agate, w_aproj, w_bgate, w_bproj, w_gate, out_gain, out_bias, w_out):
    block_size = 64
    valid = token_valid.astype(jnp.float32)

    def project(carried):
        pair_block, valid_block = carried
        normed = layer_norm(pair_block.astype(jnp.float32), ln_gain, ln_bias).astype(jnp.bfloat16)
        normed_wide = normed.astype(jnp.float32)

        def linear(weight):
            return jnp.einsum('crq,cd->drq', normed_wide, weight.astype(jnp.float32))
        pair_mask = (valid_block[:, None] * valid[None, :])[None, :, :]
        left_side = (jax.nn.sigmoid(linear(w_agate)) * linear(w_aproj) * pair_mask).astype(jnp.bfloat16)
        right_side = (jax.nn.sigmoid(linear(w_bgate)) * linear(w_bproj) * pair_mask).astype(jnp.bfloat16)
        gate_value = jax.nn.sigmoid(linear(w_gate)).astype(jnp.bfloat16)
        return (left_side, right_side, gate_value)
    blocks = pair.reshape(C, N // block_size, block_size, N).transpose(1, 0, 2, 3)
    left_side, right_side, gate_value = lax.map(project, (blocks, valid.reshape(N // block_size, block_size)))
    left_chan = left_side.transpose(1, 0, 2, 3).reshape(C // 8, 8, N, N)
    right_chan = right_side.transpose(1, 0, 2, 3).reshape(C // 8, 8, N, N)
    gate_value = gate_value.transpose(1, 0, 2, 3).reshape(C, N, N)

    def triangle(carried):
        left_block, right_block = carried
        return jnp.einsum('cik,cjk->cij', left_block.astype(jnp.float32), right_block.astype(jnp.float32))
    mixed = lax.map(triangle, (left_chan, right_chan)).reshape(C, N, N)
    centre = lax.optimization_barrier(jnp.mean(mixed, axis=0))
    square_mean = lax.optimization_barrier(jnp.mean(mixed * mixed, axis=0))
    spread_sq = square_mean - centre * centre
    normed_mixed = ((mixed - centre) * lax.rsqrt(spread_sq + EPSILON) * out_gain[:, None, None] + out_bias[:, None, None]).astype(jnp.bfloat16)
    projected = jnp.einsum('cij,cd->dij', normed_mixed.astype(jnp.float32), w_out.astype(jnp.float32))
    return (gate_value.astype(jnp.float32) * projected).astype(jnp.bfloat16)
```

```python
import jax
import jax.numpy as jnp
from jax import lax
from jax.experimental import pallas as pl
from jax.experimental.pallas import tpu as pltpu
from jax.sharding import PartitionSpec as P

EPSILON = 1e-05
MESH = pl.DeviceIdType.MESH
F32 = jnp.float32
BF16 = jnp.bfloat16
NT = (((1,), (1,)), ((), ()))


def device_at(x, y, z, core):
    return ((y * 2 + z % 2) * 2 + core, x, z // 2)


def wait_bytes(ref, sem):
    pltpu.make_async_copy(ref, ref, sem).wait()


def remote(src, dst, send_sem, recv_sem, device):
    return pltpu.make_async_remote_copy(
        src, dst, send_sem, recv_sem, device_id=device, device_id_type=MESH
    )


def rows_of(block):
    return block.astype(F32).reshape(-1, 128).astype(BF16)


def one_hot(shape, offset):
    first = lax.broadcasted_iota(jnp.int32, shape, 0)
    second = lax.broadcasted_iota(jnp.int32, shape, 1)
    return (second == first + offset).astype(F32).astype(BF16)


def centred(blocks, scratch, gain=None, shift=None):
    def add(step, total):
        part = blocks[step].astype(F32)
        return total + jnp.sum(part, axis=0)

    centre = lax.fori_loop(0, 8, add, jnp.zeros((8, 128), F32)) * (1.0 / 128)

    def add_square(step, total):
        part = blocks[step].astype(F32) - centre
        return total + jnp.sum(part * part, axis=0)

    spread = lax.fori_loop(0, 8, add_square, jnp.zeros((8, 128), F32)) * (1.0 / 128)
    scale = lax.rsqrt(spread + EPSILON)

    def put(step, _):
        for member in range(16):
            c = step * 16 + member
            value = (blocks[step, member].astype(F32) - centre) * scale
            if gain is not None:
                value = value * gain[c] + shift[c]
            scratch[pl.ds(pl.multiple_of(c * 8, 8), 8), :] = value
        return 0

    lax.fori_loop(0, 8, put, 0)


def by_channel(scratch, out):
    def put(step, _):
        for member in range(16):
            out[step, member] = scratch[pl.ds(step * 16 + member, 8, stride=128), :].astype(BF16)
        return 0

    lax.fori_loop(0, 8, put, 0)


def kernel(
    pair, valid_row, valid_s_in, gain_in, bias_in, w0, w1, w2, w3, w4, out_gain_in, out_bias_in, w_out_in,
    out,
    xin, valid_v, valid_s, gain_s, bias_s, out_gain_s, out_bias_s, w_v, w_out_v, w_all, w_out_t,
    edge, edge_all,
    wide, left_f, right_f, gate_f,
    left_send, left_mid, left_all, right_send, right_mid, right_all,
    mixed_send, mixed_mid, mixed_all, out_send,
    load_sem, send_sem, recv_sem, own_sem, sibling_send, right_recv, sibling_recv,
):
    row, x, z_hi = lax.axis_index("row"), lax.axis_index("col"), lax.axis_index("chan")
    core, z_lo, y = row % 2, (row // 2) % 2, row // 4
    z = z_hi * 2 + z_lo
    xy = y * 4 + x

    def z_peer(t):
        return lax.rem(z + t, 8)

    def hi_peer(t):
        return lax.rem(z_hi + t, 4)

    def xy_peer(t):
        px, py = lax.rem(x + t % 4, 4), lax.rem(y + t // 4, 4)
        return px, py

    def at_z(pz):
        return device_at(x, y, pz, core)

    def at_hi(ph):
        return (row, x, ph)

    def at_xy(px, py):
        return device_at(px, py, z, core)

    sibling = device_at(x, y, z, 1 - core)

    barrier = pltpu.get_barrier_semaphore()

    def greet_z(t, _):
        pl.semaphore_signal(barrier, inc=1, device_id=at_z(z_peer(t)), device_id_type=MESH)
        return 0

    def greet_xy(t, _):
        pl.semaphore_signal(barrier, inc=1, device_id=at_xy(*xy_peer(t)), device_id_type=MESH)
        return 0

    lax.fori_loop(1, 8, greet_z, 0)
    lax.fori_loop(1, 16, greet_xy, 0)
    pl.semaphore_signal(barrier, inc=1, device_id=sibling, device_id_type=MESH)

    own_rows = pltpu.make_async_copy(pair.at[:, :, z_hi], xin.at[pl.ds(z_hi * 2, 2)], load_sem.at[0])
    own_rows.start()
    weight_loads = []
    for t, w in enumerate((w0, w1, w2, w3, w4)):
        weight_loads.append(pltpu.make_async_copy(w, w_v.at[t], load_sem.at[1 + t]))
    weight_loads.append(pltpu.make_async_copy(w_out_in, w_out_v, load_sem.at[6]))
    small_loads = [
        pltpu.make_async_copy(valid_row, valid_v, load_sem.at[7]),
        pltpu.make_async_copy(valid_s_in, valid_s, load_sem.at[8]),
        pltpu.make_async_copy(gain_in, gain_s, load_sem.at[9]),
        pltpu.make_async_copy(bias_in, bias_s, load_sem.at[10]),
        pltpu.make_async_copy(out_gain_in, out_gain_s, load_sem.at[11]),
        pltpu.make_async_copy(out_bias_in, out_bias_s, load_sem.at[12]),
    ]
    for copy in weight_loads + small_loads:
        copy.start()

    pl.semaphore_wait(barrier, 23)

    for t in (2, 1, 3):
        ph = hi_peer(t)
        remote(
            pair.at[:, :, ph], xin.at[pl.ds(z_hi * 2, 2)], send_sem.at[0], recv_sem.at[0], at_hi(ph)
        ).start()

    for copy in weight_loads + small_loads:
        copy.wait()
    pick = one_hot((16, 32), x * 8)
    for t in range(5):
        turned = lax.dot_general(pick, w_v[t], NT, preferred_element_type=F32)
        w_all[t, z_hi, x] = turned[0:8].astype(BF16)
    lane = lax.broadcasted_iota(jnp.int32, (8, 128), 1)
    line = lax.broadcasted_iota(jnp.int32, (8, 128), 0)

    def put_edge(i, held):
        value = jnp.where(line == 0, out_gain_s[i], out_bias_s[i])
        return jnp.where(lane == z_hi * 32 + i, value, held)

    edge[...] = lax.fori_loop(0, 32, put_edge, jnp.zeros((8, 128), F32))
    for t in (1, 2, 3):
        ph = hi_peer(t)
        remote(
            w_all.at[:, z_hi, x], w_all.at[:, z_hi, x], send_sem.at[1], recv_sem.at[1], at_hi(ph)
        ).start()
        remote(edge, edge_all.at[z_hi], send_sem.at[2], recv_sem.at[2], at_hi(ph)).start()
    edge_all[z_hi] = edge[...]
    w_out_t[...] = lax.dot_general(
        one_hot((128, 128), 0), w_out_v[...], NT, preferred_element_type=F32
    ).astype(BF16)
    wait_bytes(w_all.at[:, 0, pl.ds(0, 3)], recv_sem.at[1])
    for t in (1, 2, 3):
        px = lax.rem(x + t, 4)
        remote(
            w_all.at[:, :, x], w_all.at[:, :, x], send_sem.at[3], recv_sem.at[3], at_xy(px, y)
        ).start()
    wait_bytes(edge_all.at[pl.ds(0, 3)], recv_sem.at[2])
    edge_sum = edge_all[0] + edge_all[1] + edge_all[2] + edge_all[3]
    out_gain = jnp.transpose(jnp.broadcast_to(edge_sum[0:1], (128, 128)))
    out_shift = jnp.transpose(jnp.broadcast_to(edge_sum[1:2], (128, 128)))

    own_rows.wait()
    wait_bytes(xin.at[pl.ds(0, 6)], recv_sem.at[0])
    centred(xin, wide, gain_s, bias_s)

    wait_bytes(w_all.at[:, :, pl.ds(0, 3)], recv_sem.at[3])
    col_valid = valid_v[pl.ds(x, 1), :].astype(F32)
    first_row = row * 32 + z_hi * 8

    def project(step, _):
        normed, masks = [], []
        for member in range(2):
            r = step * 2 + member
            normed.append(wide[pl.ds(r, 128, stride=8), :].astype(BF16))
            masks.append(col_valid * valid_s[first_row + r].astype(F32))
        normed = jnp.concatenate(normed, axis=1)
        mask = jnp.concatenate(masks, axis=1)

        def linear(t):
            return jnp.dot(rows_of(w_all[t]), normed, preferred_element_type=F32)

        left = jax.nn.sigmoid(linear(0)) * linear(1) * mask
        right = jax.nn.sigmoid(linear(2)) * linear(3) * mask
        gate = jax.nn.sigmoid(linear(4)).astype(BF16).astype(F32)
        for member in range(2):
            at = pl.ds(pl.multiple_of((step * 2 + member) * 128, 128), 128)
            lanes = slice(member * 128, member * 128 + 128)
            left_f[at, :] = left[:, lanes]
            right_f[at, :] = right[:, lanes]
            gate_f[at, :] = gate[:, lanes]
        return 0

    lax.fori_loop(0, 4, project, 0)
    by_channel(right_f, right_send)

    def send_right(t, _):
        px, py = xy_peer(t)
        remote(
            right_send.at[:, py * 4 + px], right_mid.at[xy], send_sem.at[4], recv_sem.at[4], at_xy(px, py)
        ).start()
        return 0

    def own(src, dst, i):
        copy = pltpu.make_async_copy(src, dst, own_sem.at[i])
        copy.start()
        return copy

    lax.fori_loop(1, 16, send_right, 0)
    own_right = own(right_send.at[:, xy], right_mid.at[xy], 0)
    by_channel(left_f, left_send)

    def send_left(t, _):
        pz = z_peer(t)
        remote(
            left_send.at[pz], left_mid.at[z], send_sem.at[5], recv_sem.at[5], at_z(pz)
        ).start()
        return 0

    lax.fori_loop(1, 8, send_left, 0)
    own_left = own(left_send.at[z], left_mid.at[z], 1)

    own_right.wait()
    wait_bytes(right_mid.at[pl.ds(0, 15)], recv_sem.at[4])

    def slot(pz, pcore):
        return (pz % 2) * 8 + pcore * 4 + pz // 2

    mine = slot(z, core)

    def pass_right(t, _):
        pz = z_peer(t)
        remote(
            right_mid.at[:, pz], right_all.at[:, mine], send_sem.at[6], right_recv.at[8 - t], at_z(pz)
        ).start()
        return 0

    lax.fori_loop(1, 8, pass_right, 0)
    own_right = own(right_mid.at[:, z], right_all.at[:, mine], 2)

    own_left.wait()
    wait_bytes(left_mid.at[pl.ds(0, 7)], recv_sem.at[5])

    def pass_left(t, _):
        px, py = xy_peer(t)
        remote(
            left_mid.at[:, py * 4 + px], left_all.at[xy], send_sem.at[7], recv_sem.at[7], at_xy(px, py)
        ).start()
        return 0

    lax.fori_loop(1, 16, pass_left, 0)
    own_left = own(left_mid.at[:, xy], left_all.at[xy], 3)

    own_right.wait()

    def to_sibling(pz):
        part = right_all.at[:, slot(pz, core)]
        remote(part, part, sibling_send, sibling_recv, sibling).start()

    to_sibling(z)

    def share(t, _):
        wait_bytes(right_all.at[:, 0], right_recv.at[t])
        to_sibling(z_peer(t))
        return 0

    lax.fori_loop(1, 8, share, 0)
    own_left.wait()
    wait_bytes(left_all.at[pl.ds(0, 15)], recv_sem.at[7])
    wait_bytes(right_all.at[:, pl.ds(0, 8)], sibling_recv)

    for part in range(4):
        total = jnp.zeros((256, 128), F32)
        for step in range(4):
            left = jnp.concatenate([rows_of(left_all[py * 4 + step]) for py in range(4)], axis=0)
            right = rows_of(right_all[part * 4 + step])
            total = total + lax.dot_general(left, right, NT, preferred_element_type=F32)
        for py in range(4):
            mixed_send[:, py * 4 + part] = (
                total[py * 64 : py * 64 + 64].reshape(8, 8, 128).astype(BF16)
            )

    def send_mixed(t, _):
        pz = z_peer(t)
        remote(
            mixed_send.at[pz], mixed_mid.at[z], send_sem.at[8], recv_sem.at[8], at_z(pz)
        ).start()
        return 0

    lax.fori_loop(1, 8, send_mixed, 0)
    own(mixed_send.at[z], mixed_mid.at[z], 4).wait()
    wait_bytes(mixed_mid.at[pl.ds(0, 7)], recv_sem.at[8])

    def pass_mixed(t, _):
        px, py = xy_peer(t)
        remote(
            mixed_mid.at[:, py * 4 + px], mixed_all.at[:, xy], send_sem.at[9], recv_sem.at[9], at_xy(px, py)
        ).start()
        return 0

    lax.fori_loop(1, 16, pass_mixed, 0)
    own(mixed_mid.at[:, xy], mixed_all.at[:, xy], 5).wait()
    wait_bytes(mixed_all.at[:, pl.ds(0, 15)], recv_sem.at[9])

    centred(mixed_all, wide)

    def finish(step, _):
        normed = []
        for member in range(2):
            r = step * 2 + member
            value = wide[pl.ds(r, 128, stride=8), :] * out_gain + out_shift
            normed.append(value.astype(BF16))
        projected = jnp.dot(
            w_out_t[...], jnp.concatenate(normed, axis=1), preferred_element_type=F32
        )
        for member in range(2):
            at = pl.ds(pl.multiple_of((step * 2 + member) * 128, 128), 128)
            left_f[at, :] = gate_f[at, :] * projected[:, member * 128 : member * 128 + 128]
        return 0

    lax.fori_loop(0, 4, finish, 0)
    by_channel(left_f, out_send)

    for t in (2, 1, 3):
        ph = hi_peer(t)
        remote(
            out_send.at[pl.ds(ph * 2, 2)], out.at[:, :, z_hi], send_sem.at[10], recv_sem.at[10], at_hi(ph)
        ).start()
    own(out_send.at[pl.ds(z_hi * 2, 2)], out.at[:, :, z_hi], 6).wait()
    wait_bytes(out.at[:, :, pl.ds(0, 3)], recv_sem.at[10])

    wait_bytes(xin.at[pl.ds(0, 6)], send_sem.at[0])
    wait_bytes(w_all.at[:, 0, pl.ds(0, 3)], send_sem.at[1])
    wait_bytes(edge_all.at[pl.ds(0, 3)], send_sem.at[2])
    wait_bytes(w_all.at[:, :, pl.ds(0, 3)], send_sem.at[3])
    wait_bytes(right_mid.at[pl.ds(0, 15)], send_sem.at[4])
    wait_bytes(left_mid.at[pl.ds(0, 7)], send_sem.at[5])
    wait_bytes(right_mid.at[:, pl.ds(0, 7)], send_sem.at[6])
    wait_bytes(left_all.at[pl.ds(0, 15)], send_sem.at[7])
    wait_bytes(mixed_mid.at[pl.ds(0, 7)], send_sem.at[8])
    wait_bytes(mixed_all.at[:, pl.ds(0, 15)], send_sem.at[9])
    wait_bytes(out.at[:, :, pl.ds(0, 3)], send_sem.at[10])
    wait_bytes(right_all.at[:, pl.ds(0, 8)], sibling_send)


def on_device(
    pair,
    token_valid,
    ln_gain,
    ln_bias,
    w_agate,
    w_aproj,
    w_bgate,
    w_bproj,
    w_gate,
    out_gain,
    out_bias,
    w_out,
):
    any_spec = pl.BlockSpec(memory_space=pl.ANY)
    result = pl.pallas_call(
        kernel,
        name="triangle",
        out_shape=jax.ShapeDtypeStruct((2, 16, 4, 8, 128), BF16),
        in_specs=[any_spec] * 13,
        out_specs=any_spec,
        scratch_shapes=[
            pltpu.VMEM((8, 16, 8, 128), BF16),
            pltpu.VMEM((4, 128), jnp.int32),
            pltpu.SMEM((512,), jnp.int32),
            pltpu.SMEM((128,), F32),
            pltpu.SMEM((128,), F32),
            pltpu.SMEM((32,), F32),
            pltpu.SMEM((32,), F32),
            pltpu.VMEM((5, 128, 32), BF16),
            pltpu.VMEM((128, 128), BF16),
            pltpu.VMEM((5, 4, 4, 8, 128), BF16),
            pltpu.VMEM((128, 128), BF16),
            pltpu.VMEM((8, 128), F32),
            pltpu.VMEM((4, 8, 128), F32),
            pltpu.VMEM((1024, 128), F32),
            pltpu.VMEM((1024, 128), F32),
            pltpu.VMEM((1024, 128), F32),
            pltpu.VMEM((1024, 128), F32),
            pltpu.VMEM((8, 16, 8, 128), BF16),
            pltpu.VMEM((8, 16, 8, 128), BF16),
            pltpu.VMEM((16, 8, 8, 128), BF16),
            pltpu.VMEM((8, 16, 8, 128), BF16),
            pltpu.VMEM((16, 8, 8, 128), BF16),
            pltpu.VMEM((16, 16, 8, 128), BF16),
            pltpu.VMEM((8, 16, 8, 128), BF16),
            pltpu.VMEM((8, 16, 8, 128), BF16),
            pltpu.VMEM((8, 16, 8, 128), BF16),
            pltpu.VMEM((8, 16, 8, 128), BF16),
            pltpu.SemaphoreType.DMA((13,)),
            pltpu.SemaphoreType.DMA((11,)),
            pltpu.SemaphoreType.DMA((11,)),
            pltpu.SemaphoreType.DMA((7,)),
            pltpu.SemaphoreType.DMA,
            pltpu.SemaphoreType.DMA((8,)),
            pltpu.SemaphoreType.DMA,
        ],
        compiler_params=pltpu.CompilerParams(
            collective_id=0, has_side_effects=True, vmem_limit_bytes=32 << 20
        ),
    )(
        pair.reshape(2, 16, 4, 8, 128),
        token_valid.reshape(4, 128),
        token_valid,
        ln_gain,
        ln_bias,
        w_agate,
        w_aproj,
        w_bgate,
        w_bproj,
        w_gate,
        out_gain,
        out_bias,
        w_out,
    )
    return result.reshape(32, 32, 128)


def solution(mesh):
    return jax.shard_map(
        on_device,
        mesh=mesh,
        in_specs=(
            P("chan", "row", "col"),
            P(),
            P(),
            P(),
            P(None, "chan"),
            P(None, "chan"),
            P(None, "chan"),
            P(None, "chan"),
            P(None, "chan"),
            P("chan"),
            P("chan"),
            P(),
        ),
        out_specs=P("chan", "row", "col"),
        check_vma=False,
    )
```

```python
import jax
import jax.numpy as jnp
from jax import lax
from jax.experimental import pallas as pl
from jax.experimental.pallas import tpu as pltpu
from jax.sharding import PartitionSpec as P

EPSILON = 1e-05
MESH = pl.DeviceIdType.MESH
F32 = jnp.float32
BF16 = jnp.bfloat16
NT = (((1,), (1,)), ((), ()))


def device_at(x, y, z, core):
    return ((y * 2 + z % 2) * 2 + core, x, z // 2)


def wait_bytes(ref, sem):
    pltpu.make_async_copy(ref, ref, sem).wait()


def remote(src, dst, send_sem, recv_sem, device):
    return pltpu.make_async_remote_copy(
        src, dst, send_sem, recv_sem, device_id=device, device_id_type=MESH
    )


def rows_of(block):
    return block.astype(F32).reshape(-1, 128).astype(BF16)


def one_hot(shape, offset):
    first = lax.broadcasted_iota(jnp.int32, shape, 0)
    second = lax.broadcasted_iota(jnp.int32, shape, 1)
    return (second == first + offset).astype(F32).astype(BF16)


def centred(blocks, scratch, gain=None, shift=None):
    def add(step, total):
        part = blocks[pl.ds(step * 16, 16)].astype(F32)
        return total + jnp.sum(part, axis=0)

    centre = lax.fori_loop(0, 8, add, jnp.zeros((8, 128), F32)) * (1.0 / 128)

    def add_square(step, total):
        part = blocks[pl.ds(step * 16, 16)].astype(F32) - centre
        return total + jnp.sum(part * part, axis=0)

    spread = lax.fori_loop(0, 8, add_square, jnp.zeros((8, 128), F32)) * (1.0 / 128)
    scale = lax.rsqrt(spread + EPSILON)

    def put(step, _):
        for member in range(16):
            c = step * 16 + member
            value = (blocks[c].astype(F32) - centre) * scale
            if gain is not None:
                value = value * gain[c] + shift[c]
            scratch[pl.ds(pl.multiple_of(c * 8, 8), 8), :] = value
        return 0

    lax.fori_loop(0, 8, put, 0)


def by_channel(scratch, out):
    def put(step, _):
        for member in range(16):
            out[step, member] = scratch[pl.ds(step * 16 + member, 8, stride=128), :].astype(BF16)
        return 0

    lax.fori_loop(0, 8, put, 0)


def kernel(
    pair, valid_row, valid_s_in, gain_in, bias_in, w0, w1, w2, w3, w4, out_gain_in, out_bias_in, w_out_in,
    out,
    xin, valid_v, valid_s, gain_s, bias_s, out_gain_s, out_bias_s, w_out_v, w_all, w_out_t,
    edge, edge_all,
    wide, left_f, right_f, gate_f,
    left_send, left_mid, left_all, right_send, right_mid, right_all,
    mixed_send, mixed_all, out_send,
    load_sem, send_sem, recv_sem, own_sem, sibling_send, right_recv, sibling_recv,
):
    row, x, z_hi = lax.axis_index("row"), lax.axis_index("col"), lax.axis_index("chan")
    core, z_lo, y = row % 2, (row // 2) % 2, row // 4
    z = z_hi * 2 + z_lo
    xy = y * 4 + x

    def z_peer(t):
        return lax.rem(z + t, 8)

    def hi_peer(t):
        return lax.rem(z_hi + t, 4)

    def xy_peer(t):
        px, py = lax.rem(x + t % 4, 4), lax.rem(y + t // 4, 4)
        return px, py

    def at_z(pz):
        return device_at(x, y, pz, core)

    def at_hi(ph):
        return (row, x, ph)

    def at_xy(px, py):
        return device_at(px, py, z, core)

    sibling = device_at(x, y, z, 1 - core)

    barrier = pltpu.get_barrier_semaphore()

    def greet_z(t, _):
        pl.semaphore_signal(barrier, inc=1, device_id=at_z(z_peer(t)), device_id_type=MESH)
        return 0

    def greet_xy(t, _):
        pl.semaphore_signal(barrier, inc=1, device_id=at_xy(*xy_peer(t)), device_id_type=MESH)
        return 0

    lax.fori_loop(1, 8, greet_z, 0)
    lax.fori_loop(1, 16, greet_xy, 0)
    pl.semaphore_signal(barrier, inc=1, device_id=sibling, device_id_type=MESH)

    own_rows = pltpu.make_async_copy(pair.at[:, z_hi], xin.at[pl.ds(z_hi * 32, 32)], load_sem.at[0])
    weight_loads = [
        pltpu.make_async_copy(w.at[x], w_all.at[t, z_hi, x], load_sem.at[1 + t])
        for t, w in enumerate((w0, w1, w2, w3, w4))
    ]
    out_loads = [
        pltpu.make_async_copy(w_out_in, w_out_v, load_sem.at[6]),
        pltpu.make_async_copy(out_gain_in, out_gain_s, load_sem.at[7]),
        pltpu.make_async_copy(out_bias_in, out_bias_s, load_sem.at[8]),
    ]
    in_loads = [
        pltpu.make_async_copy(valid_row, valid_v, load_sem.at[9]),
        pltpu.make_async_copy(valid_s_in, valid_s, load_sem.at[10]),
        pltpu.make_async_copy(gain_in, gain_s, load_sem.at[11]),
        pltpu.make_async_copy(bias_in, bias_s, load_sem.at[12]),
    ]
    for copy in weight_loads + out_loads + in_loads + [own_rows]:
        copy.start()
    for copy in weight_loads + out_loads:
        copy.wait()
    lane = lax.broadcasted_iota(jnp.int32, (8, 128), 1)
    line = lax.broadcasted_iota(jnp.int32, (8, 128), 0)

    def put_edge(i, held):
        value = jnp.where(line == 0, out_gain_s[i], out_bias_s[i])
        return jnp.where(lane == z_hi * 32 + i, value, held)

    edge[...] = lax.fori_loop(0, 32, put_edge, jnp.zeros((8, 128), F32))
    edge_all[z_hi] = edge[...]
    w_out_t[...] = lax.dot_general(
        one_hot((128, 128), 0), w_out_v[...], NT, preferred_element_type=F32
    ).astype(BF16)

    pl.semaphore_wait(barrier, 23)

    for t in (2, 1, 3):
        ph = hi_peer(t)
        remote(
            w_all.at[:, z_hi, x], w_all.at[:, z_hi, x], send_sem.at[1], recv_sem.at[1], at_hi(ph)
        ).start()
    for t in (2, 1, 3):
        ph = hi_peer(t)
        remote(
            pair.at[:, ph], xin.at[pl.ds(z_hi * 32, 32)], send_sem.at[0], recv_sem.at[0], at_hi(ph)
        ).start()
    for t in (2, 1, 3):
        ph = hi_peer(t)
        remote(edge, edge_all.at[z_hi], send_sem.at[2], recv_sem.at[2], at_hi(ph)).start()
    for copy in in_loads:
        copy.wait()
    wait_bytes(w_all.at[:, 0, pl.ds(0, 3)], recv_sem.at[1])
    for t in (2, 1, 3):
        px = lax.rem(x + t, 4)
        remote(
            w_all.at[:, :, x], w_all.at[:, :, x], send_sem.at[3], recv_sem.at[3], at_xy(px, y)
        ).start()

    own_rows.wait()
    wait_bytes(xin.at[pl.ds(0, 96)], recv_sem.at[0])
    centred(xin, wide, gain_s, bias_s)

    wait_bytes(w_all.at[:, :, pl.ds(0, 3)], recv_sem.at[3])
    col_valid = valid_v[pl.ds(x, 1), :].astype(F32)
    first_row = row * 32 + z_hi * 8

    def rows_at(step):
        normed = [wide[pl.ds(step * 2 + member, 128, stride=8), :].astype(BF16) for member in range(2)]
        return jnp.concatenate(normed, axis=1)

    def linear(t, normed):
        return jnp.dot(rows_of(w_all[t]), normed, preferred_element_type=F32)

    def put_rows(ref, step, value):
        for member in range(2):
            at = pl.ds(pl.multiple_of((step * 2 + member) * 128, 128), 128)
            ref[at, :] = value[:, member * 128 : member * 128 + 128]

    def edges(first, ref):
        def project(step, _):
            normed = rows_at(step)
            masks = [
                col_valid * valid_s[first_row + step * 2 + member].astype(F32) for member in range(2)
            ]
            value = jax.nn.sigmoid(linear(first, normed)) * linear(first + 1, normed)
            put_rows(ref, step, value * jnp.concatenate(masks, axis=1))
            return 0

        lax.fori_loop(0, 4, project, 0)

    def gates(step, _):
        value = jax.nn.sigmoid(linear(4, rows_at(step)))
        put_rows(gate_f, step, value.astype(BF16).astype(F32))
        return 0

    edges(2, right_f)
    by_channel(right_f, right_send)

    def send_right(t, _):
        px, py = xy_peer(t)
        remote(
            right_send.at[:, py * 4 + px], right_mid.at[xy], send_sem.at[4], recv_sem.at[4], at_xy(px, py)
        ).start()
        return 0

    def own(src, dst, i):
        copy = pltpu.make_async_copy(src, dst, own_sem.at[i])
        copy.start()
        return copy

    lax.fori_loop(1, 16, send_right, 0)
    own_right = own(right_send.at[:, xy], right_mid.at[xy], 0)
    edges(0, left_f)
    by_channel(left_f, left_send)

    def send_left(t, _):
        pz = z_peer(t)
        remote(
            left_send.at[pz], left_mid.at[z], send_sem.at[5], recv_sem.at[5], at_z(pz)
        ).start()
        return 0

    lax.fori_loop(1, 8, send_left, 0)
    own_left = own(left_send.at[z], left_mid.at[z], 1)

    own_right.wait()
    wait_bytes(right_mid.at[pl.ds(0, 15)], recv_sem.at[4])

    def slot(pz, pcore):
        return (pz % 2) * 8 + pcore * 4 + pz // 2

    mine = slot(z, core)

    def pass_right(t, _):
        pz = z_peer(t)
        remote(
            right_mid.at[:, pz], right_all.at[:, mine], send_sem.at[6], right_recv.at[8 - t], at_z(pz)
        ).start()
        return 0

    lax.fori_loop(1, 8, pass_right, 0)
    own_right = own(right_mid.at[:, z], right_all.at[:, mine], 2)

    own_left.wait()
    wait_bytes(left_mid.at[pl.ds(0, 7)], recv_sem.at[5])

    def pass_left(t, _):
        px, py = xy_peer(t)
        remote(
            left_mid.at[:, py * 4 + px], left_all.at[xy], send_sem.at[7], recv_sem.at[7], at_xy(px, py)
        ).start()
        return 0

    lax.fori_loop(1, 16, pass_left, 0)
    own_left = own(left_mid.at[:, xy], left_all.at[xy], 3)

    lax.fori_loop(0, 4, gates, 0)

    own_right.wait()

    def to_sibling(pz):
        part = right_all.at[:, slot(pz, core)]
        remote(part, part, sibling_send, sibling_recv, sibling).start()

    to_sibling(z)

    def share(t, _):
        wait_bytes(right_all.at[:, 0], right_recv.at[t])
        to_sibling(z_peer(t))
        return 0

    lax.fori_loop(1, 8, share, 0)
    own_left.wait()
    wait_bytes(left_all.at[pl.ds(0, 15)], recv_sem.at[7])
    wait_bytes(right_all.at[:, pl.ds(0, 8)], sibling_recv)

    wait_bytes(edge_all.at[pl.ds(0, 3)], recv_sem.at[2])

    for part in range(4):
        total = jnp.zeros((256, 128), F32)
        for step in range(4):
            left = jnp.concatenate([rows_of(left_all[py * 4 + step]) for py in range(4)], axis=0)
            right = rows_of(right_all[part * 4 + step])
            total = total + lax.dot_general(left, right, NT, preferred_element_type=F32)
        for py in range(4):
            mixed_send[:, py * 4 + part] = (
                total[py * 64 : py * 64 + 64].reshape(8, 8, 128).astype(BF16)
            )

    def send_mixed(t, _):
        i, q = t // 16, t % 16
        away = lax.rem(4 + (1 - 2 * (i % 2)) * ((i + 1) // 2) + 8, 8)
        pz = lax.rem(z + away, 8)
        px, py = lax.rem(x + 2 + q % 4, 4), lax.rem(y + 2 + q // 4, 4)
        remote(
            mixed_send.at[pz, py * 4 + px], mixed_all.at[z * 16 + xy], send_sem.at[8], recv_sem.at[8],
            device_at(px, py, pz, core),
        ).start()
        return 0

    lax.fori_loop(0, 122, send_mixed, 0)
    lax.fori_loop(123, 128, send_mixed, 0)
    own(mixed_send.at[z, xy], mixed_all.at[z * 16 + xy], 4).wait()
    wait_bytes(mixed_all.at[pl.ds(0, 127)], recv_sem.at[8])

    centred(mixed_all, wide)
    edge_sum = edge_all[0] + edge_all[1] + edge_all[2] + edge_all[3]
    out_gain = jnp.transpose(jnp.broadcast_to(edge_sum[0:1], (128, 128)))
    out_shift = jnp.transpose(jnp.broadcast_to(edge_sum[1:2], (128, 128)))

    def finish(step, _):
        normed = []
        for member in range(2):
            r = step * 2 + member
            value = wide[pl.ds(r, 128, stride=8), :] * out_gain + out_shift
            normed.append(value.astype(BF16))
        projected = jnp.dot(
            w_out_t[...], jnp.concatenate(normed, axis=1), preferred_element_type=F32
        )
        for member in range(2):
            at = pl.ds(pl.multiple_of((step * 2 + member) * 128, 128), 128)
            left_f[at, :] = gate_f[at, :] * projected[:, member * 128 : member * 128 + 128]
        return 0

    lax.fori_loop(0, 4, finish, 0)
    by_channel(left_f, out_send)

    for t in (2, 1, 3):
        ph = hi_peer(t)
        remote(
            out_send.at[pl.ds(ph * 2, 2)], out.at[:, :, z_hi], send_sem.at[10], recv_sem.at[10], at_hi(ph)
        ).start()
    own(out_send.at[pl.ds(z_hi * 2, 2)], out.at[:, :, z_hi], 6).wait()
    wait_bytes(out.at[:, :, pl.ds(0, 3)], recv_sem.at[10])

    wait_bytes(xin.at[pl.ds(0, 96)], send_sem.at[0])
    wait_bytes(w_all.at[:, 0, pl.ds(0, 3)], send_sem.at[1])
    wait_bytes(edge_all.at[pl.ds(0, 3)], send_sem.at[2])
    wait_bytes(w_all.at[:, :, pl.ds(0, 3)], send_sem.at[3])
    wait_bytes(right_mid.at[pl.ds(0, 15)], send_sem.at[4])
    wait_bytes(left_mid.at[pl.ds(0, 7)], send_sem.at[5])
    wait_bytes(right_mid.at[:, pl.ds(0, 7)], send_sem.at[6])
    wait_bytes(left_all.at[pl.ds(0, 15)], send_sem.at[7])
    wait_bytes(mixed_all.at[pl.ds(0, 127)], send_sem.at[8])
    wait_bytes(out.at[:, :, pl.ds(0, 3)], send_sem.at[10])
    wait_bytes(right_all.at[:, pl.ds(0, 8)], sibling_send)


def on_device(
    pair,
    token_valid,
    ln_gain,
    ln_bias,
    w_agate,
    w_aproj,
    w_bgate,
    w_bproj,
    w_gate,
    out_gain,
    out_bias,
    w_out,
):
    any_spec = pl.BlockSpec(memory_space=pltpu.HBM)
    result = pl.pallas_call(
        kernel,
        name="triangle",
        out_shape=jax.ShapeDtypeStruct((2, 16, 4, 8, 128), BF16),
        in_specs=[any_spec] * 13,
        out_specs=any_spec,
        scratch_shapes=[
            pltpu.VMEM((128, 8, 128), BF16),
            pltpu.VMEM((4, 128), jnp.int32),
            pltpu.SMEM((512,), jnp.int32),
            pltpu.SMEM((128,), F32),
            pltpu.SMEM((128,), F32),
            pltpu.SMEM((32,), F32),
            pltpu.SMEM((32,), F32),
                pltpu.VMEM((128, 128), BF16),
            pltpu.VMEM((5, 4, 4, 8, 128), BF16),
            pltpu.VMEM((128, 128), BF16),
            pltpu.VMEM((8, 128), F32),
            pltpu.VMEM((4, 8, 128), F32),
            pltpu.VMEM((1024, 128), F32),
            pltpu.VMEM((1024, 128), F32),
            pltpu.VMEM((1024, 128), F32),
            pltpu.VMEM((1024, 128), F32),
            pltpu.VMEM((8, 16, 8, 128), BF16),
            pltpu.VMEM((8, 16, 8, 128), BF16),
            pltpu.VMEM((16, 8, 8, 128), BF16),
            pltpu.VMEM((8, 16, 8, 128), BF16),
            pltpu.VMEM((16, 8, 8, 128), BF16),
            pltpu.VMEM((16, 16, 8, 128), BF16),
            pltpu.VMEM((8, 16, 8, 128), BF16),
            pltpu.VMEM((128, 8, 128), BF16),
            pltpu.VMEM((8, 16, 8, 128), BF16),
            pltpu.SemaphoreType.DMA((13,)),
            pltpu.SemaphoreType.DMA((11,)),
            pltpu.SemaphoreType.DMA((11,)),
            pltpu.SemaphoreType.DMA((7,)),
            pltpu.SemaphoreType.DMA,
            pltpu.SemaphoreType.DMA((8,)),
            pltpu.SemaphoreType.DMA,
        ],
        compiler_params=pltpu.CompilerParams(
            collective_id=0, has_side_effects=True, vmem_limit_bytes=62 << 20
        ),
    )(
        pair.reshape(32, 4, 8, 128),
        token_valid.reshape(4, 128),
        token_valid,
        ln_gain,
        ln_bias,
        w_agate.T.reshape(4, 8, 128),
        w_aproj.T.reshape(4, 8, 128),
        w_bgate.T.reshape(4, 8, 128),
        w_bproj.T.reshape(4, 8, 128),
        w_gate.T.reshape(4, 8, 128),
        out_gain,
        out_bias,
        w_out,
    )
    return result.reshape(32, 32, 128)


def solution(mesh):
    return jax.shard_map(
        on_device,
        mesh=mesh,
        in_specs=(
            P("chan", "row", "col"),
            P(),
            P(),
            P(),
            P(None, "chan"),
            P(None, "chan"),
            P(None, "chan"),
            P(None, "chan"),
            P(None, "chan"),
            P("chan"),
            P("chan"),
            P(),
        ),
        out_specs=P("chan", "row", "col"),
        check_vma=False,
    )
```

```python
import jax
import jax.numpy as jnp
from jax import lax
from jax.experimental import pallas as pl
from jax.experimental.pallas import tpu as pltpu
from jax.sharding import PartitionSpec as P

EPSILON = 1e-05
MESH = pl.DeviceIdType.MESH
F32 = jnp.float32
BF16 = jnp.bfloat16
NT = (((1,), (1,)), ((), ()))
Z_AWAY = (4, 3, 5, 2, 6, 1, 7, 0)
MIRROR = (0, 2, 1, 4, 3, 6, 5, 7)
GROUPS = ((0, 1, 2), (3, 4, 5, 6, 7))


def device_at(x, y, z, core):
    return ((y * 2 + z % 2) * 2 + core, x, z // 2)


def wait_bytes(ref, sem):
    pltpu.make_async_copy(ref, ref, sem).wait()


def remote(src, dst, send_sem, recv_sem, device):
    return pltpu.make_async_remote_copy(
        src, dst, send_sem, recv_sem, device_id=device, device_id_type=MESH
    )


def rows_of(block):
    return block.astype(F32).reshape(-1, 128).astype(BF16)


def one_hot(shape, offset):
    first = lax.broadcasted_iota(jnp.int32, shape, 0)
    second = lax.broadcasted_iota(jnp.int32, shape, 1)
    return (second == first + offset).astype(F32).astype(BF16)


def centred(blocks, scratch, gain=None, shift=None):
    def add(step, total):
        part = blocks[pl.ds(step * 16, 16)].astype(F32)
        return total + jnp.sum(part, axis=0)

    centre = lax.fori_loop(0, 8, add, jnp.zeros((8, 128), F32)) * (1.0 / 128)

    def add_square(step, total):
        part = blocks[pl.ds(step * 16, 16)].astype(F32) - centre
        return total + jnp.sum(part * part, axis=0)

    spread = lax.fori_loop(0, 8, add_square, jnp.zeros((8, 128), F32)) * (1.0 / 128)
    scale = lax.rsqrt(spread + EPSILON)

    def put(step, _):
        for member in range(16):
            c = step * 16 + member
            value = (blocks[c].astype(F32) - centre) * scale
            if gain is not None:
                value = value * gain[c] + shift[c]
            scratch[pl.ds(pl.multiple_of(c * 8, 8), 8), :] = value
        return 0

    lax.fori_loop(0, 8, put, 0)


def by_channel(scratch, out, first=0, count=8):
    def put(step, _):
        for member in range(16):
            out[step, member] = scratch[pl.ds(step * 16 + member, 8, stride=128), :].astype(BF16)
        return 0

    lax.fori_loop(first, first + count, put, 0)


def kernel(
    pair, valid_row, valid_s_in, gain_in, bias_in, w0, w1, w2, w3, w4, out_gain_in, out_bias_in, w_out_in,
    out,
    xin, valid_v, valid_s, gain_s, bias_s, out_gain_s, out_bias_s, w_out_v, w_all, w_out_t,
    edge, edge_all,
    wide, left_f, right_f, gate_f,
    left_send, left_all, right_send, right_all, mixed_send, mixed_all, out_send,
    load_sem, send_sem, recv_sem, own_sem, sibling_send, left_recv, right_recv, sibling_recv, plane_sem,
):
    row, x, z_hi = lax.axis_index("row"), lax.axis_index("col"), lax.axis_index("chan")
    core, z_lo, y = row % 2, (row // 2) % 2, row // 4
    z = z_hi * 2 + z_lo
    xy = y * 4 + x

    def hi_peer(t):
        return (z_hi + t) % 4

    def at_hi(ph):
        return (row, x, ph)

    sibling = device_at(x, y, z, 1 - core)
    z_peers = [(z + away) % 8 for away in Z_AWAY]

    barrier = pltpu.get_barrier_semaphore()
    for pz in z_peers[:7]:
        pl.semaphore_signal(
            barrier, inc=1, device_id=device_at(x, y, pz, core), device_id_type=MESH
        )

    def greet_xy(t, _):
        pl.semaphore_signal(
            barrier,
            inc=1,
            device_id=device_at((x + t % 4) % 4, (y + t // 4) % 4, z, core),
            device_id_type=MESH,
        )
        return 0

    lax.fori_loop(1, 16, greet_xy, 0)
    pl.semaphore_signal(barrier, inc=1, device_id=sibling, device_id_type=MESH)

    half = pl.ds(core * 2, 2)
    own_rows = pltpu.make_async_copy(pair.at[:, z_hi], xin.at[pl.ds(z_hi * 32, 32)], load_sem.at[0])
    weight_loads = [
        pltpu.make_async_copy(w.at[x], w_all.at[t, z_hi, x], load_sem.at[1 + t])
        for t, w in enumerate((w0, w1, w2))
    ] + [
        pltpu.make_async_copy(w.at[half], w_all.at[3 + t, z_hi, half], load_sem.at[4 + t])
        for t, w in enumerate((w3, w4))
    ]
    out_loads = [
        pltpu.make_async_copy(w_out_in, w_out_v, load_sem.at[6]),
        pltpu.make_async_copy(out_gain_in, out_gain_s, load_sem.at[7]),
        pltpu.make_async_copy(out_bias_in, out_bias_s, load_sem.at[8]),
    ]
    in_loads = [
        pltpu.make_async_copy(valid_row, valid_v, load_sem.at[9]),
        pltpu.make_async_copy(valid_s_in, valid_s, load_sem.at[10]),
        pltpu.make_async_copy(gain_in, gain_s, load_sem.at[11]),
        pltpu.make_async_copy(bias_in, bias_s, load_sem.at[12]),
    ]
    for copy in weight_loads + out_loads + in_loads + [own_rows]:
        copy.start()
    for copy in weight_loads + out_loads:
        copy.wait()
    lane = lax.broadcasted_iota(jnp.int32, (8, 128), 1)
    line = lax.broadcasted_iota(jnp.int32, (8, 128), 0)

    def put_edge(i, held):
        value = jnp.where(line == 0, out_gain_s[i], out_bias_s[i])
        return jnp.where(lane == z_hi * 32 + i, value, held)

    edge[...] = lax.fori_loop(0, 32, put_edge, jnp.zeros((8, 128), F32))
    edge_all[z_hi] = edge[...]
    w_out_t[...] = lax.dot_general(
        one_hot((128, 128), 0), w_out_v[...], NT, preferred_element_type=F32
    ).astype(BF16)

    pl.semaphore_wait(barrier, 23)

    right_weights = w_all.at[pl.ds(3, 2), z_hi, half]
    left_weights = w_all.at[pl.ds(0, 3), z_hi, x]
    for t in (2, 1, 3):
        ph = hi_peer(t)
        remote(right_weights, right_weights, send_sem.at[1], recv_sem.at[1], at_hi(ph)).start()
    for t in (2, 1, 3):
        ph = hi_peer(t)
        remote(left_weights, left_weights, send_sem.at[9], recv_sem.at[9], at_hi(ph)).start()
    for t in (2, 1, 3):
        ph = hi_peer(t)
        remote(
            pair.at[:, ph], xin.at[pl.ds(z_hi * 32, 32)], send_sem.at[0], recv_sem.at[0], at_hi(ph)
        ).start()
    for pz in z_peers[:7]:
        pl.semaphore_signal(
            plane_sem, inc=1, device_id=device_at(x, y, pz, core), device_id_type=MESH
        )
    for t in (2, 1, 3):
        ph = hi_peer(t)
        remote(edge, edge_all.at[z_hi], send_sem.at[2], recv_sem.at[2], at_hi(ph)).start()
    for copy in in_loads:
        copy.wait()
    wait_bytes(w_all.at[pl.ds(3, 2), pl.ds(0, 3), pl.ds(0, 2)], recv_sem.at[1])
    right_weights = w_all.at[pl.ds(3, 2), :, half]
    remote(right_weights, right_weights, send_sem.at[4], recv_sem.at[4], sibling).start()
    wait_bytes(w_all.at[pl.ds(0, 3), pl.ds(0, 3), 0], recv_sem.at[9])
    left_weights = w_all.at[pl.ds(0, 3), :, x]
    for t in (2, 1, 3):
        remote(
            left_weights, left_weights, send_sem.at[3], recv_sem.at[3],
            device_at((x + t) % 4, y, z, core),
        ).start()

    own_rows.wait()
    wait_bytes(xin.at[pl.ds(0, 96)], recv_sem.at[0])
    centred(xin, wide, gain_s, bias_s)

    wait_bytes(w_all.at[pl.ds(3, 2), :, pl.ds(0, 2)], recv_sem.at[4])
    col_valid = valid_v[pl.ds(x, 1), :].astype(F32)
    first_row = row * 32 + z_hi * 8

    def rows_at(step):
        normed = [wide[pl.ds(step * 2 + member, 128, stride=8), :].astype(BF16) for member in range(2)]
        return jnp.concatenate(normed, axis=1)

    def linear(t, normed):
        return jnp.dot(rows_of(w_all[t]), normed, preferred_element_type=F32)

    def put_rows(ref, step, value):
        for member in range(2):
            at = pl.ds(pl.multiple_of((step * 2 + member) * 128, 128), 128)
            ref[at, :] = value[:, member * 128 : member * 128 + 128]

    def edges(first, ref):
        def project(step, _):
            normed = rows_at(step)
            masks = [
                col_valid * valid_s[first_row + step * 2 + member].astype(F32) for member in range(2)
            ]
            value = jax.nn.sigmoid(linear(first, normed)) * linear(first + 1, normed)
            put_rows(ref, step, value * jnp.concatenate(masks, axis=1))
            return 0

        lax.fori_loop(0, 4, project, 0)

    def gates(step, _):
        value = jax.nn.sigmoid(linear(2, rows_at(step)))
        put_rows(gate_f, step, value.astype(BF16).astype(F32))
        return 0

    def own(src, dst, i):
        copy = pltpu.make_async_copy(src, dst, own_sem.at[i])
        copy.start()
        return copy

    def xy_peer(k):
        px, py = (x + 2 + k % 4) % 4, (y + 2 + k // 4) % 4
        return px, py, py * 4 + px

    def to_all(start, places):
        def plane(k, _):
            px, py, pxy = xy_peer(k)
            for i in places:
                if i < 7:
                    start(i, px, py, pxy)
                else:
                    pl.when(k != 10)(lambda: start(7, px, py, pxy))
            return 0

        lax.fori_loop(0, 16, plane, 0)

    edges(3, right_f)
    by_channel(right_f, right_send)
    pl.semaphore_wait(plane_sem, 7)

    def slot(pz, pcore):
        return (pz % 2) * 8 + pcore * 4 + pz // 2

    mine = slot(z, core)

    def send_right(i, px, py, pxy):
        remote(
            right_send.at[z_peers[i], pxy], right_all.at[xy, mine],
            send_sem.at[5], right_recv.at[MIRROR[i]], device_at(px, py, z_peers[i], core),
        ).start()

    to_all(send_right, range(8))
    own_right = own(right_send.at[z, xy], right_all.at[xy, mine], 0)

    wait_bytes(w_all.at[pl.ds(0, 3), :, pl.ds(0, 3)], recv_sem.at[3])
    edges(0, left_f)
    by_channel(left_f, left_send)

    def send_left(i, px, py, pxy):
        remote(
            left_send.at[z_peers[i], pxy], left_all.at[x, MIRROR[i], y],
            send_sem.at[6], left_recv.at[MIRROR[i]], device_at(px, py, z_peers[i], core),
        ).start()

    to_all(send_left, range(8))
    own_left = own(left_send.at[z, xy], left_all.at[x, 7, y], 1)
    lax.fori_loop(0, 4, gates, 0)

    for i in range(8):
        if i == 7:
            own_right.wait()
            wait_bytes(right_all.at[pl.ds(0, 15), 0], right_recv.at[7])
        else:
            wait_bytes(right_all.at[:, 0], right_recv.at[i])
        part = right_all.at[:, slot(z_peers[i], core)]
        remote(part, part, sibling_send, sibling_recv, sibling).start()
    wait_bytes(right_all.at[:, pl.ds(0, 8)], sibling_recv)
    wait_bytes(edge_all.at[pl.ds(0, 3)], recv_sem.at[2])

    def send_mixed(i, px, py, pxy):
        remote(
            mixed_send.at[i, pxy], mixed_all.at[z * 16 + xy], send_sem.at[7], recv_sem.at[7],
            device_at(px, py, z_peers[i], core),
        ).start()

    for group in GROUPS:
        first, count = group[0], len(group)
        for i in group:
            if i == 7:
                own_left.wait()
                wait_bytes(right_all.at[pl.ds(0, 15), 0], left_recv.at[7])
            else:
                wait_bytes(left_all.at[:, 0], left_recv.at[i])
        left = jnp.concatenate(
            [rows_of(left_all[step, pl.ds(first, count)]) for step in range(4)], axis=1
        )
        for part in range(4):
            right = jnp.concatenate([rows_of(right_all[part * 4 + step]) for step in range(4)], axis=1)
            total = lax.dot_general(left, right, NT, preferred_element_type=F32)
            total = total.reshape(count, 4, 8, 128).astype(BF16)
            for py in range(4):
                mixed_send[pl.ds(first, count), py * 4 + part] = total[:, py]
        to_all(send_mixed, group)
    own(mixed_send.at[7, xy], mixed_all.at[z * 16 + xy], 2).wait()
    wait_bytes(mixed_all.at[pl.ds(0, 127)], recv_sem.at[7])

    centred(mixed_all, wide)
    edge_sum = edge_all[0] + edge_all[1] + edge_all[2] + edge_all[3]
    out_gain = jnp.transpose(jnp.broadcast_to(edge_sum[0:1], (128, 128)))
    out_shift = jnp.transpose(jnp.broadcast_to(edge_sum[1:2], (128, 128)))

    def finish(step, _):
        normed = []
        for member in range(2):
            r = step * 2 + member
            value = wide[pl.ds(r, 128, stride=8), :] * out_gain + out_shift
            normed.append(value.astype(BF16))
        projected = jnp.dot(
            w_out_t[...], jnp.concatenate(normed, axis=1), preferred_element_type=F32
        )
        for member in range(2):
            at = pl.ds(pl.multiple_of((step * 2 + member) * 128, 128), 128)
            left_f[at, :] = gate_f[at, :] * projected[:, member * 128 : member * 128 + 128]
        return 0

    lax.fori_loop(0, 4, finish, 0)

    for t in (2, 1, 3, 0):
        ph = hi_peer(t)
        part = out_send.at[pl.ds(ph * 2, 2)]
        by_channel(left_f, out_send, ph * 2, 2)
        if t:
            remote(part, out.at[:, :, z_hi], send_sem.at[8], recv_sem.at[8], at_hi(ph)).start()
        else:
            own(part, out.at[:, :, z_hi], 3).wait()
    wait_bytes(out.at[:, :, pl.ds(0, 3)], recv_sem.at[8])

    wait_bytes(xin.at[pl.ds(0, 96)], send_sem.at[0])
    wait_bytes(w_all.at[pl.ds(3, 2), pl.ds(0, 3), pl.ds(0, 2)], send_sem.at[1])
    wait_bytes(edge_all.at[pl.ds(0, 3)], send_sem.at[2])
    wait_bytes(w_all.at[pl.ds(0, 3), :, pl.ds(0, 3)], send_sem.at[3])
    wait_bytes(w_all.at[pl.ds(3, 2), :, pl.ds(0, 2)], send_sem.at[4])
    wait_bytes(mixed_all.at[pl.ds(0, 127)], send_sem.at[5])
    wait_bytes(mixed_all.at[pl.ds(0, 127)], send_sem.at[6])
    wait_bytes(mixed_all.at[pl.ds(0, 127)], send_sem.at[7])
    wait_bytes(out.at[:, :, pl.ds(0, 3)], send_sem.at[8])
    wait_bytes(w_all.at[pl.ds(0, 3), pl.ds(0, 3), 0], send_sem.at[9])
    wait_bytes(right_all.at[:, pl.ds(0, 8)], sibling_send)


def on_device(
    pair,
    token_valid,
    ln_gain,
    ln_bias,
    w_agate,
    w_aproj,
    w_bgate,
    w_bproj,
    w_gate,
    out_gain,
    out_bias,
    w_out,
):
    any_spec = pl.BlockSpec(memory_space=pltpu.HBM)
    operands = [
        pltpu.with_memory_space_constraint(array, pltpu.HBM)
        for array in (
            pair.reshape(32, 4, 8, 128),
            token_valid.reshape(4, 128),
            token_valid,
            ln_gain,
            ln_bias,
            w_agate.T.reshape(4, 8, 128),
            w_aproj.T.reshape(4, 8, 128),
            w_gate.T.reshape(4, 8, 128),
            w_bgate.T.reshape(4, 8, 128),
            w_bproj.T.reshape(4, 8, 128),
            out_gain,
            out_bias,
            w_out,
        )
    ]
    result = pl.pallas_call(
        kernel,
        name="triangle",
        out_shape=pltpu.VMEM((2, 16, 4, 8, 128), BF16),
        in_specs=[any_spec] * 13,
        out_specs=pl.BlockSpec(memory_space=pl.ANY),
        scratch_shapes=[
            pltpu.VMEM((128, 8, 128), BF16),
            pltpu.VMEM((4, 128), jnp.int32),
            pltpu.SMEM((512,), jnp.int32),
            pltpu.SMEM((128,), F32),
            pltpu.SMEM((128,), F32),
            pltpu.SMEM((32,), F32),
            pltpu.SMEM((32,), F32),
                pltpu.VMEM((128, 128), BF16),
            pltpu.VMEM((5, 4, 4, 8, 128), BF16),
            pltpu.VMEM((128, 128), BF16),
            pltpu.VMEM((8, 128), F32),
            pltpu.VMEM((4, 8, 128), F32),
            pltpu.VMEM((1024, 128), F32),
            pltpu.VMEM((1024, 128), F32),
            pltpu.VMEM((1024, 128), F32),
            pltpu.VMEM((1024, 128), F32),
            pltpu.VMEM((8, 16, 8, 128), BF16),
            pltpu.VMEM((4, 8, 4, 8, 128), BF16),
            pltpu.VMEM((8, 16, 8, 128), BF16),
            pltpu.VMEM((16, 16, 8, 128), BF16),
            pltpu.VMEM((8, 16, 8, 128), BF16),
            pltpu.VMEM((128, 8, 128), BF16),
            pltpu.VMEM((8, 16, 8, 128), BF16),
            pltpu.SemaphoreType.DMA((13,)),
            pltpu.SemaphoreType.DMA((10,)),
            pltpu.SemaphoreType.DMA((10,)),
            pltpu.SemaphoreType.DMA((4,)),
            pltpu.SemaphoreType.DMA,
            pltpu.SemaphoreType.DMA((8,)),
            pltpu.SemaphoreType.DMA((8,)),
            pltpu.SemaphoreType.DMA,
            pltpu.SemaphoreType.REGULAR,
        ],
        compiler_params=pltpu.CompilerParams(
            collective_id=0, has_side_effects=True, vmem_limit_bytes=32 << 20
        ),
    )(*operands)
    return result.reshape(32, 32, 128)


def solution(mesh):
    return jax.shard_map(
        on_device,
        mesh=mesh,
        in_specs=(
            P("chan", "row", "col"),
            P(),
            P(),
            P(),
            P(None, "chan"),
            P(None, "chan"),
            P(None, "chan"),
            P(None, "chan"),
            P(None, "chan"),
            P("chan"),
            P("chan"),
            P(),
        ),
        out_specs=P("chan", "row", "col"),
        check_vma=False,
    )
```

```python
import jax
import jax.numpy as jnp
from jax import lax
from jax.experimental import pallas as pl
from jax.experimental.pallas import tpu as pltpu
from jax.sharding import PartitionSpec as P

EPSILON = 1e-05
MESH = pl.DeviceIdType.MESH
F32 = jnp.float32
BF16 = jnp.bfloat16
NT = (((1,), (1,)), ((), ()))
Z_AWAY = (4, 3, 5, 2, 6, 1, 7, 0)
MIRROR = (0, 2, 1, 4, 3, 6, 5, 7)
GROUPS = ((0,1,2),(3,4),(5,6,7))


def device_at(x, y, z, core):
    return ((y * 2 + z % 2) * 2 + core, x, z // 2)


def wait_bytes(ref, sem):
    pltpu.make_async_copy(ref, ref, sem).wait()


def remote(src, dst, send_sem, recv_sem, device):
    return pltpu.make_async_remote_copy(
        src, dst, send_sem, recv_sem, device_id=device, device_id_type=MESH
    )


def rows_of(block):
    return block.astype(F32).reshape(-1, 128).astype(BF16)


def one_hot(shape, offset):
    first = lax.broadcasted_iota(jnp.int32, shape, 0)
    second = lax.broadcasted_iota(jnp.int32, shape, 1)
    return (second == first + offset).astype(F32).astype(BF16)


def centred(blocks, scratch, gain=None, shift=None):
    def add(step, total):
        part = blocks[pl.ds(step * 16, 16)].astype(F32)
        return total + jnp.sum(part, axis=0)

    centre = lax.fori_loop(0, 8, add, jnp.zeros((8, 128), F32)) * (1.0 / 128)

    def add_square(step, total):
        part = blocks[pl.ds(step * 16, 16)].astype(F32) - centre
        return total + jnp.sum(part * part, axis=0)

    spread = lax.fori_loop(0, 8, add_square, jnp.zeros((8, 128), F32)) * (1.0 / 128)
    scale = lax.rsqrt(spread + EPSILON)

    def put(step, _):
        for member in range(16):
            c = step * 16 + member
            value = (blocks[c].astype(F32) - centre) * scale
            if gain is not None:
                value = value * gain[c] + shift[c]
            scratch[pl.ds(pl.multiple_of(c * 8, 8), 8), :] = value
        return 0

    lax.fori_loop(0, 8, put, 0)


def by_channel(scratch, out, first=0, count=8):
    def put(step, _):
        for member in range(16):
            out[step, member] = scratch[pl.ds(step * 16 + member, 8, stride=128), :].astype(BF16)
        return 0

    lax.fori_loop(first, first + count, put, 0)


def kernel(
    pair, valid_row, valid_s_in, gain_in, bias_in, w0, w1, w2, w3, w4, out_gain_in, out_bias_in, w_out_in,
    out,
    xin, valid_v, valid_s, gain_s, bias_s, out_gain_s, out_bias_s, w_out_v, w_all, w_out_t,
    edge, edge_all,
    wide, left_f, right_f, gate_f,
    left_send, left_all, right_send, right_all, mixed_send, mixed_all, out_send,
    load_sem, send_sem, recv_sem, own_sem, sibling_send, left_recv, right_recv, sibling_recv, plane_sem,
):
    row, x, z_hi = lax.axis_index("row"), lax.axis_index("col"), lax.axis_index("chan")
    core, z_lo, y = row % 2, (row // 2) % 2, row // 4
    z = z_hi * 2 + z_lo
    xy = y * 4 + x

    def hi_peer(t):
        return (z_hi + t) % 4

    def at_hi(ph):
        return (row, x, ph)

    sibling = device_at(x, y, z, 1 - core)
    z_peers = [(z + away) % 8 for away in Z_AWAY]

    barrier = pltpu.get_barrier_semaphore()
    for pz in z_peers[:7]:
        pl.semaphore_signal(
            barrier, inc=1, device_id=device_at(x, y, pz, core), device_id_type=MESH
        )

    def greet_xy(t, _):
        pl.semaphore_signal(
            barrier,
            inc=1,
            device_id=device_at((x + t % 4) % 4, (y + t // 4) % 4, z, core),
            device_id_type=MESH,
        )
        return 0

    lax.fori_loop(1, 16, greet_xy, 0)
    pl.semaphore_signal(barrier, inc=1, device_id=sibling, device_id_type=MESH)

    half = pl.ds(core * 2, 2)
    own_rows = pltpu.make_async_copy(pair.at[:, z_hi], xin.at[pl.ds(z_hi * 32, 32)], load_sem.at[0])
    weight_loads = [
        pltpu.make_async_copy(w.at[x], w_all.at[t, z_hi, x], load_sem.at[1 + t])
        for t, w in enumerate((w0, w1, w2))
    ] + [
        pltpu.make_async_copy(w.at[half], w_all.at[3 + t, z_hi, half], load_sem.at[4 + t])
        for t, w in enumerate((w3, w4))
    ]
    out_loads = [
        pltpu.make_async_copy(w_out_in, w_out_v, load_sem.at[6]),
        pltpu.make_async_copy(out_gain_in, out_gain_s, load_sem.at[7]),
        pltpu.make_async_copy(out_bias_in, out_bias_s, load_sem.at[8]),
    ]
    in_loads = [
        pltpu.make_async_copy(valid_row, valid_v, load_sem.at[9]),
        pltpu.make_async_copy(valid_s_in, valid_s, load_sem.at[10]),
        pltpu.make_async_copy(gain_in, gain_s, load_sem.at[11]),
        pltpu.make_async_copy(bias_in, bias_s, load_sem.at[12]),
    ]
    for copy in weight_loads + out_loads + in_loads + [own_rows]:
        copy.start()
    for copy in weight_loads + out_loads:
        copy.wait()
    lane = lax.broadcasted_iota(jnp.int32, (8, 128), 1)
    line = lax.broadcasted_iota(jnp.int32, (8, 128), 0)

    def put_edge(i, held):
        value = jnp.where(line == 0, out_gain_s[i], out_bias_s[i])
        return jnp.where(lane == z_hi * 32 + i, value, held)

    edge[...] = lax.fori_loop(0, 32, put_edge, jnp.zeros((8, 128), F32))
    edge_all[z_hi] = edge[...]
    w_out_t[...] = lax.dot_general(
        one_hot((128, 128), 0), w_out_v[...], NT, preferred_element_type=F32
    ).astype(BF16)

    pl.semaphore_wait(barrier, 23)

    right_weights = w_all.at[pl.ds(3, 2), z_hi, half]
    left_weights = w_all.at[pl.ds(0, 3), z_hi, x]
    for t in (2, 1, 3):
        ph = hi_peer(t)
        remote(right_weights, right_weights, send_sem.at[1], recv_sem.at[1], at_hi(ph)).start()
    for t in (2, 1, 3):
        ph = hi_peer(t)
        remote(left_weights, left_weights, send_sem.at[9], recv_sem.at[9], at_hi(ph)).start()
    for t in (2, 1, 3):
        ph = hi_peer(t)
        remote(
            pair.at[:, ph], xin.at[pl.ds(z_hi * 32, 32)], send_sem.at[0], recv_sem.at[0], at_hi(ph)
        ).start()
    for pz in z_peers[:7]:
        pl.semaphore_signal(
            plane_sem, inc=1, device_id=device_at(x, y, pz, core), device_id_type=MESH
        )
    for t in (2, 1, 3):
        ph = hi_peer(t)
        remote(edge, edge_all.at[z_hi], send_sem.at[2], recv_sem.at[2], at_hi(ph)).start()
    for copy in in_loads:
        copy.wait()
    wait_bytes(w_all.at[pl.ds(3, 2), pl.ds(0, 3), pl.ds(0, 2)], recv_sem.at[1])
    right_weights = w_all.at[pl.ds(3, 2), :, half]
    remote(right_weights, right_weights, send_sem.at[4], recv_sem.at[4], sibling).start()
    wait_bytes(w_all.at[pl.ds(0, 3), pl.ds(0, 3), 0], recv_sem.at[9])
    left_weights = w_all.at[pl.ds(0, 3), :, x]
    for t in (2, 1, 3):
        remote(
            left_weights, left_weights, send_sem.at[3], recv_sem.at[3],
            device_at((x + t) % 4, y, z, core),
        ).start()

    own_rows.wait()
    wait_bytes(xin.at[pl.ds(0, 96)], recv_sem.at[0])
    centred(xin, wide, gain_s, bias_s)

    wait_bytes(w_all.at[pl.ds(3, 2), :, pl.ds(0, 2)], recv_sem.at[4])
    col_valid = valid_v[pl.ds(x, 1), :].astype(F32)
    first_row = row * 32 + z_hi * 8

    def rows_at(step):
        normed = [wide[pl.ds(step * 2 + member, 128, stride=8), :].astype(BF16) for member in range(2)]
        return jnp.concatenate(normed, axis=1)

    def linear(t, normed):
        return jnp.dot(rows_of(w_all[t]), normed, preferred_element_type=F32)

    def put_rows(ref, step, value):
        for member in range(2):
            at = pl.ds(pl.multiple_of((step * 2 + member) * 128, 128), 128)
            ref[at, :] = value[:, member * 128 : member * 128 + 128]

    def edges(first, ref):
        def project(step, _):
            normed = rows_at(step)
            masks = [
                col_valid * valid_s[first_row + step * 2 + member].astype(F32) for member in range(2)
            ]
            value = jax.nn.sigmoid(linear(first, normed)) * linear(first + 1, normed)
            put_rows(ref, step, value * jnp.concatenate(masks, axis=1))
            return 0

        lax.fori_loop(0, 4, project, 0, unroll=True)

    def gates(step, _):
        value = jax.nn.sigmoid(linear(2, rows_at(step)))
        put_rows(gate_f, step, value.astype(BF16).astype(F32))
        return 0

    def own(src, dst, i):
        copy = pltpu.make_async_copy(src, dst, own_sem.at[i])
        copy.start()
        return copy

    def to_all(start, places):
        for i in places:
            def line(j, _):
                py = (y + 2 + j) % 4
                for m in range(4):
                    px = (x + 2 + m) % 4
                    if i < 7 or m != 2:
                        start(i, px, py, py * 4 + px)
                    else:
                        pl.when(j != 2)(lambda: start(i, px, py, py * 4 + px))
                return 0

            lax.fori_loop(0, 4, line, 0)

    edges(3, right_f)
    by_channel(right_f, right_send)
    pl.semaphore_wait(plane_sem, 7)

    def slot(pz, pcore):
        return (pz % 2) * 8 + pcore * 4 + pz // 2

    mine = slot(z, core)

    def send_right(i, px, py, pxy):
        remote(
            right_send.at[z_peers[i], pxy], right_all.at[xy, mine],
            send_sem.at[5], right_recv.at[MIRROR[i]], device_at(px, py, z_peers[i], core),
        ).start()

    to_all(send_right, range(8))
    own_right = own(right_send.at[z, xy], right_all.at[xy, mine], 0)

    wait_bytes(w_all.at[pl.ds(0, 3), :, pl.ds(0, 3)], recv_sem.at[3])
    edges(0, left_f)
    by_channel(left_f, left_send)

    def send_left(i, px, py, pxy):
        remote(
            left_send.at[z_peers[i], pxy], left_all.at[x, MIRROR[i], y],
            send_sem.at[6], left_recv.at[MIRROR[i]], device_at(px, py, z_peers[i], core),
        ).start()

    to_all(send_left, range(8))
    own_left = own(left_send.at[z, xy], left_all.at[x, 7, y], 1)
    lax.fori_loop(0, 4, gates, 0, unroll=True)

    for i in range(8):
        if i == 7:
            own_right.wait()
            wait_bytes(right_all.at[pl.ds(0, 15), 0], right_recv.at[7])
        else:
            wait_bytes(right_all.at[:, 0], right_recv.at[i])
        part = right_all.at[:, slot(z_peers[i], core)]
        remote(part, part, sibling_send, sibling_recv, sibling).start()
    wait_bytes(right_all.at[:, pl.ds(0, 8)], sibling_recv)
    wait_bytes(edge_all.at[pl.ds(0, 3)], recv_sem.at[2])

    def send_mixed(i, px, py, pxy):
        remote(
            mixed_send.at[i, pxy], mixed_all.at[z * 16 + xy], send_sem.at[7], recv_sem.at[7],
            device_at(px, py, z_peers[i], core),
        ).start()

    for group in GROUPS:
        first, count = group[0], len(group)
        for i in group:
            if i == 7:
                own_left.wait()
                wait_bytes(right_all.at[pl.ds(0, 15), 0], left_recv.at[7])
            else:
                wait_bytes(left_all.at[:, 0], left_recv.at[i])
        left = jnp.concatenate(
            [rows_of(left_all[step, pl.ds(first, count)]) for step in range(4)], axis=1
        )
        for part in range(4):
            right = jnp.concatenate([rows_of(right_all[part * 4 + step]) for step in range(4)], axis=1)
            total = lax.dot_general(left, right, NT, preferred_element_type=F32)
            total = total.reshape(count, 4, 8, 128).astype(BF16)
            for py in range(4):
                mixed_send[pl.ds(first, count), py * 4 + part] = total[:, py]
        to_all(send_mixed, group)
    own(mixed_send.at[7, xy], mixed_all.at[z * 16 + xy], 2).wait()
    wait_bytes(mixed_all.at[pl.ds(0, 127)], recv_sem.at[7])

    centred(mixed_all, wide)
    edge_sum = edge_all[0] + edge_all[1] + edge_all[2] + edge_all[3]
    out_gain = jnp.transpose(jnp.broadcast_to(edge_sum[0:1], (128, 128)))
    out_shift = jnp.transpose(jnp.broadcast_to(edge_sum[1:2], (128, 128)))

    def finish(step, _):
        normed = []
        for member in range(2):
            r = step * 2 + member
            value = wide[pl.ds(r, 128, stride=8), :] * out_gain + out_shift
            normed.append(value.astype(BF16))
        projected = jnp.dot(
            w_out_t[...], jnp.concatenate(normed, axis=1), preferred_element_type=F32
        )
        for member in range(2):
            at = pl.ds(pl.multiple_of((step * 2 + member) * 128, 128), 128)
            left_f[at, :] = gate_f[at, :] * projected[:, member * 128 : member * 128 + 128]
        return 0

    lax.fori_loop(0, 4, finish, 0, unroll=True)

    for t in (2, 1, 3, 0):
        ph = hi_peer(t)
        part = out_send.at[pl.ds(ph * 2, 2)]
        by_channel(left_f, out_send, ph * 2, 2)
        if t:
            remote(part, out.at[:, :, z_hi], send_sem.at[8], recv_sem.at[8], at_hi(ph)).start()
        else:
            own(part, out.at[:, :, z_hi], 3).wait()
    wait_bytes(out.at[:, :, pl.ds(0, 3)], recv_sem.at[8])

    wait_bytes(xin.at[pl.ds(0, 96)], send_sem.at[0])
    wait_bytes(w_all.at[pl.ds(3, 2), pl.ds(0, 3), pl.ds(0, 2)], send_sem.at[1])
    wait_bytes(edge_all.at[pl.ds(0, 3)], send_sem.at[2])
    wait_bytes(w_all.at[pl.ds(0, 3), :, pl.ds(0, 3)], send_sem.at[3])
    wait_bytes(w_all.at[pl.ds(3, 2), :, pl.ds(0, 2)], send_sem.at[4])
    wait_bytes(mixed_all.at[pl.ds(0, 127)], send_sem.at[5])
    wait_bytes(mixed_all.at[pl.ds(0, 127)], send_sem.at[6])
    wait_bytes(mixed_all.at[pl.ds(0, 127)], send_sem.at[7])
    wait_bytes(out.at[:, :, pl.ds(0, 3)], send_sem.at[8])
    wait_bytes(w_all.at[pl.ds(0, 3), pl.ds(0, 3), 0], send_sem.at[9])
    wait_bytes(right_all.at[:, pl.ds(0, 8)], sibling_send)


def on_device(
    pair,
    token_valid,
    ln_gain,
    ln_bias,
    w_agate,
    w_aproj,
    w_bgate,
    w_bproj,
    w_gate,
    out_gain,
    out_bias,
    w_out,
):
    any_spec = pl.BlockSpec(memory_space=pltpu.HBM)
    operands = [
        pltpu.with_memory_space_constraint(array, pltpu.HBM)
        for array in (
            pair.reshape(32, 4, 8, 128),
            token_valid.reshape(4, 128),
            token_valid,
            ln_gain,
            ln_bias,
            w_agate.T.reshape(4, 8, 128),
            w_aproj.T.reshape(4, 8, 128),
            w_gate.T.reshape(4, 8, 128),
            w_bgate.T.reshape(4, 8, 128),
            w_bproj.T.reshape(4, 8, 128),
            out_gain,
            out_bias,
            w_out,
        )
    ]
    result = pl.pallas_call(
        kernel,
        name="triangle",
        out_shape=pltpu.VMEM((2, 16, 4, 8, 128), BF16),
        in_specs=[any_spec] * 13,
        out_specs=pl.BlockSpec(memory_space=pl.ANY),
        scratch_shapes=[
            pltpu.VMEM((128, 8, 128), BF16),
            pltpu.VMEM((4, 128), jnp.int32),
            pltpu.SMEM((512,), jnp.int32),
            pltpu.SMEM((128,), F32),
            pltpu.SMEM((128,), F32),
            pltpu.SMEM((32,), F32),
            pltpu.SMEM((32,), F32),
                pltpu.VMEM((128, 128), BF16),
            pltpu.VMEM((5, 4, 4, 8, 128), BF16),
            pltpu.VMEM((128, 128), BF16),
            pltpu.VMEM((8, 128), F32),
            pltpu.VMEM((4, 8, 128), F32),
            pltpu.VMEM((1024, 128), F32),
            pltpu.VMEM((1024, 128), F32),
            pltpu.VMEM((1024, 128), F32),
            pltpu.VMEM((1024, 128), F32),
            pltpu.VMEM((8, 16, 8, 128), BF16),
            pltpu.VMEM((4, 8, 4, 8, 128), BF16),
            pltpu.VMEM((8, 16, 8, 128), BF16),
            pltpu.VMEM((16, 16, 8, 128), BF16),
            pltpu.VMEM((8, 16, 8, 128), BF16),
            pltpu.VMEM((128, 8, 128), BF16),
            pltpu.VMEM((8, 16, 8, 128), BF16),
            pltpu.SemaphoreType.DMA((13,)),
            pltpu.SemaphoreType.DMA((10,)),
            pltpu.SemaphoreType.DMA((10,)),
            pltpu.SemaphoreType.DMA((4,)),
            pltpu.SemaphoreType.DMA,
            pltpu.SemaphoreType.DMA((8,)),
            pltpu.SemaphoreType.DMA((8,)),
            pltpu.SemaphoreType.DMA,
            pltpu.SemaphoreType.REGULAR,
        ],
        compiler_params=pltpu.CompilerParams(
            collective_id=0, has_side_effects=True, vmem_limit_bytes=32 << 20
        ),
    )(*operands)
    return result.reshape(32, 32, 128)


def solution(mesh):
    return jax.shard_map(
        on_device,
        mesh=mesh,
        in_specs=(
            P("chan", "row", "col"),
            P(),
            P(),
            P(),
            P(None, "chan"),
            P(None, "chan"),
            P(None, "chan"),
            P(None, "chan"),
            P(None, "chan"),
            P("chan"),
            P("chan"),
            P(),
        ),
        out_specs=P("chan", "row", "col"),
        check_vma=False,
    )
```

```python
import jax
import jax.numpy as jnp
from jax import lax
from jax.experimental import pallas as pl
from jax.experimental.pallas import tpu as pltpu
from jax.sharding import PartitionSpec as P

EPSILON = 1e-05
MESH = pl.DeviceIdType.MESH
F32 = jnp.float32
BF16 = jnp.bfloat16
NT = (((1,), (1,)), ((), ()))
Z_AWAY = (4, 3, 5, 2, 6, 1, 7, 0)
MIRROR = (0, 2, 1, 4, 3, 6, 5, 7)
GROUPS = ((0, 1, 2), (3, 4), (5, 6, 7))


def device_at(x, y, z, core):
    return ((y * 2 + z % 2) * 2 + core, x, z // 2)


def wait_bytes(ref, sem):
    pltpu.make_async_copy(ref, ref, sem).wait()


def remote(src, dst, send_sem, recv_sem, device):
    return pltpu.make_async_remote_copy(
        src, dst, send_sem, recv_sem, device_id=device, device_id_type=MESH
    )


def rows_of(block):
    return block.astype(F32).reshape(-1, 128).astype(BF16)


def one_hot(shape, offset):
    first = lax.broadcasted_iota(jnp.int32, shape, 0)
    second = lax.broadcasted_iota(jnp.int32, shape, 1)
    return (second == first + offset).astype(F32).astype(BF16)


def centred(blocks, scratch, gain=None, shift=None):
    n = blocks.shape[1]

    def add(step, total):
        part = blocks[pl.ds(step * 16, 16)].astype(F32)
        return total + jnp.sum(part, axis=0)

    centre = lax.fori_loop(0, 8, add, jnp.zeros((n, 128), F32)) * (1.0 / 128)

    def add_square(step, total):
        part = blocks[pl.ds(step * 16, 16)].astype(F32) - centre
        return total + jnp.sum(part * part, axis=0)

    spread = lax.fori_loop(0, 8, add_square, jnp.zeros((n, 128), F32)) * (1.0 / 128)
    scale = lax.rsqrt(spread + EPSILON)

    def put(step, _):
        for member in range(16):
            c = step * 16 + member
            value = (blocks[c].astype(F32) - centre) * scale
            if gain is not None:
                value = value * gain[c] + shift[c]
            scratch[pl.ds(pl.multiple_of(c * n, n), n), :] = value
        return 0

    lax.fori_loop(0, 8, put, 0)


def by_channel(scratch, out, first=0, count=8, base=0):
    n = out.shape[2]

    def put(step, _):
        for member in range(16):
            out[step, member] = scratch[pl.ds(base + step * 16 + member, n, stride=128), :].astype(BF16)
        return 0

    lax.fori_loop(first, first + count, put, 0)


def kernel(
    pair, valid_row, valid_s_in, gain_in, bias_in, w0, w1, w2, w3, w4, out_gain_in, out_bias_in, w_out_in,
    out,
    xin, valid_v, valid_s, gain_s, bias_s, out_gain_s, out_bias_s, w_out_v, w_all, w_out_t,
    edge, edge_all,
    wide, left_f, right_f, gate_f,
    left_send, left_all, right_send, right_all, mixed_send, mixed_all, out_send,
    load_sem, send_sem, recv_sem, own_sem, sibling_send, left_recv, right_recv, sibling_recv, mixed_recv, out_sem, plane_sem,
):
    row, x, z_hi = lax.axis_index("row"), lax.axis_index("col"), lax.axis_index("chan")
    core, z_lo, y = row % 2, (row // 2) % 2, row // 4
    z = z_hi * 2 + z_lo
    xy = y * 4 + x

    def hi_peer(t):
        return (z_hi + t + core * (4 - 2 * t)) % 4

    def at_hi(ph):
        return (row, x, ph)

    sibling = device_at(x, y, z, 1 - core)
    z_peers = [(z + away + core * (8 - 2 * away)) % 8 for away in Z_AWAY]

    barrier = pltpu.get_barrier_semaphore()
    for pz in z_peers[:7]:
        pl.semaphore_signal(
            barrier, inc=1, device_id=device_at(x, y, pz, core), device_id_type=MESH
        )

    def greet_xy(t, _):
        pl.semaphore_signal(
            barrier,
            inc=1,
            device_id=device_at((x + t % 4) % 4, (y + t // 4) % 4, z, core),
            device_id_type=MESH,
        )
        return 0

    lax.fori_loop(1, 16, greet_xy, 0)
    pl.semaphore_signal(barrier, inc=1, device_id=sibling, device_id_type=MESH)

    half = pl.ds(core * 2, 2)
    own_rows = pltpu.make_async_copy(pair.at[:, z_hi], xin.at[pl.ds(z_hi * 32, 32)], load_sem.at[0])
    weight_loads = [
        pltpu.make_async_copy(w.at[x], w_all.at[t, z_hi, x], load_sem.at[1 + t])
        for t, w in enumerate((w0, w1, w2))
    ] + [
        pltpu.make_async_copy(w.at[half], w_all.at[3 + t, z_hi, half], load_sem.at[4 + t])
        for t, w in enumerate((w3, w4))
    ]
    out_loads = [
        pltpu.make_async_copy(w_out_in, w_out_v, load_sem.at[6]),
        pltpu.make_async_copy(out_gain_in, out_gain_s, load_sem.at[7]),
        pltpu.make_async_copy(out_bias_in, out_bias_s, load_sem.at[8]),
    ]
    in_loads = [
        pltpu.make_async_copy(valid_row, valid_v, load_sem.at[9]),
        pltpu.make_async_copy(valid_s_in, valid_s, load_sem.at[10]),
        pltpu.make_async_copy(gain_in, gain_s, load_sem.at[11]),
        pltpu.make_async_copy(bias_in, bias_s, load_sem.at[12]),
    ]
    for copy in weight_loads + out_loads + in_loads + [own_rows]:
        copy.start()
    for copy in weight_loads + out_loads:
        copy.wait()
    lane = lax.broadcasted_iota(jnp.int32, (8, 128), 1)
    line = lax.broadcasted_iota(jnp.int32, (8, 128), 0)

    def put_edge(i, held):
        value = jnp.where(line == 0, out_gain_s[i], out_bias_s[i])
        return jnp.where(lane == z_hi * 32 + i, value, held)

    edge[...] = lax.fori_loop(0, 32, put_edge, jnp.zeros((8, 128), F32))
    edge_all[z_hi] = edge[...]
    w_out_t[...] = lax.dot_general(
        one_hot((128, 128), 0), w_out_v[...], NT, preferred_element_type=F32
    ).astype(BF16)

    pl.semaphore_wait(barrier, 23)

    right_weights = w_all.at[pl.ds(3, 2), z_hi, half]
    left_weights = w_all.at[pl.ds(0, 3), z_hi, x]
    for t in (2, 1, 3):
        ph = hi_peer(t)
        remote(right_weights, right_weights, send_sem.at[1], recv_sem.at[1], at_hi(ph)).start()
    for t in (2, 1, 3):
        ph = hi_peer(t)
        remote(left_weights, left_weights, send_sem.at[9], recv_sem.at[9], at_hi(ph)).start()
    for t in (2, 1, 3):
        ph = hi_peer(t)
        remote(
            pair.at[:, ph], xin.at[pl.ds(z_hi * 32, 32)], send_sem.at[0], recv_sem.at[0], at_hi(ph)
        ).start()
    for pz in z_peers[:7]:
        pl.semaphore_signal(
            plane_sem, inc=1, device_id=device_at(x, y, pz, core), device_id_type=MESH
        )
    for t in (2, 1, 3):
        ph = hi_peer(t)
        remote(edge, edge_all.at[z_hi], send_sem.at[2], recv_sem.at[2], at_hi(ph)).start()
    for copy in in_loads:
        copy.wait()
    wait_bytes(w_all.at[pl.ds(3, 2), pl.ds(0, 3), pl.ds(0, 2)], recv_sem.at[1])
    right_weights = w_all.at[pl.ds(3, 2), :, half]
    remote(right_weights, right_weights, send_sem.at[4], recv_sem.at[4], sibling).start()
    wait_bytes(w_all.at[pl.ds(0, 3), pl.ds(0, 3), 0], recv_sem.at[9])
    left_weights = w_all.at[pl.ds(0, 3), :, x]
    for t in (2, 1, 3):
        remote(
            left_weights, left_weights, send_sem.at[3], recv_sem.at[3],
            device_at((x + t) % 4, y, z, core),
        ).start()

    own_rows.wait()
    wait_bytes(xin.at[pl.ds(0, 96)], recv_sem.at[0])
    centred(xin, wide, gain_s, bias_s)

    wait_bytes(w_all.at[pl.ds(3, 2), :, pl.ds(0, 2)], recv_sem.at[4])
    col_valid = valid_v[pl.ds(x, 1), :].astype(F32)
    first_row = row * 32 + z_hi * 8

    def rows_at(step):
        normed = [wide[pl.ds(step * 2 + member, 128, stride=8), :].astype(BF16) for member in range(2)]
        return jnp.concatenate(normed, axis=1)

    def linear(t, normed):
        return jnp.dot(rows_of(w_all[t]), normed, preferred_element_type=F32)

    def put_rows(ref, step, value):
        for member in range(2):
            at = pl.ds(pl.multiple_of((step * 2 + member) * 128, 128), 128)
            ref[at, :] = value[:, member * 128 : member * 128 + 128]

    def edges(first, ref):
        def project(step, _):
            normed = rows_at(step)
            masks = [
                col_valid * valid_s[first_row + step * 2 + member].astype(F32) for member in range(2)
            ]
            value = jax.nn.sigmoid(linear(first, normed)) * linear(first + 1, normed)
            put_rows(ref, step, value * jnp.concatenate(masks, axis=1))
            return 0

        lax.fori_loop(0, 4, project, 0, unroll=True)

    def gates(step, _):
        value = jax.nn.sigmoid(linear(2, rows_at(step)))
        put_rows(gate_f, step, value.astype(BF16).astype(F32))
        return 0

    def own(src, dst, i):
        copy = pltpu.make_async_copy(src, dst, own_sem.at[i])
        copy.start()
        return copy

    def to_all(start, places, prepare=None):
        for i in places:
            if prepare is not None:
                prepare(z_peers[i])

            def line(j, _):
                py = (y + 2 + j + core * (4 - 2 * j)) % 4
                for m in range(4):
                    px = (x + 2 + m + core * (4 - 2 * m)) % 4
                    if i < 7 or m != 2:
                        start(i, px, py, py * 4 + px)
                    else:
                        pl.when(j != 2)(lambda: start(i, px, py, py * 4 + px))
                return 0

            lax.fori_loop(0, 4, line, 0)

    edges(3, right_f)
    pl.semaphore_wait(plane_sem, 7)

    def slot(pz, pcore):
        return (pz % 2) * 8 + pcore * 4 + pz // 2

    mine = slot(z, core)

    def send_right(i, px, py, pxy):
        remote(
            right_send.at[z_peers[i], pxy], right_all.at[xy, mine],
            send_sem.at[5], right_recv.at[MIRROR[i]], device_at(px, py, z_peers[i], core),
        ).start()

    to_all(send_right, range(8), lambda pz: by_channel(right_f, right_send, pz, 1))
    own_right = own(right_send.at[z, xy], right_all.at[xy, mine], 0)

    wait_bytes(w_all.at[pl.ds(0, 3), :, pl.ds(0, 3)], recv_sem.at[3])
    edges(0, left_f)

    def send_left(i, px, py, pxy):
        remote(
            left_send.at[z_peers[i], pxy], left_all.at[x, MIRROR[i], y],
            send_sem.at[6], left_recv.at[MIRROR[i]], device_at(px, py, z_peers[i], core),
        ).start()

    to_all(send_left, range(8), lambda pz: by_channel(left_f, left_send, pz, 1))
    own_left = own(left_send.at[z, xy], left_all.at[x, 7, y], 1)
    lax.fori_loop(0, 4, gates, 0, unroll=True)

    for i in range(8):
        if i == 7:
            own_right.wait()
            wait_bytes(right_all.at[pl.ds(0, 15), 0], right_recv.at[7])
        else:
            wait_bytes(right_all.at[:, 0], right_recv.at[i])
        part = right_all.at[:, slot(z_peers[i], core)]
        remote(part, part, sibling_send, sibling_recv, sibling).start()
    wait_bytes(right_all.at[:, pl.ds(0, 8)], sibling_recv)

    def send_mixed(part):
        def start(i, px, py, pxy):
            remote(
                mixed_send.at[part, i, pxy], mixed_all.at[part, z * 16 + xy],
                send_sem.at[7], mixed_recv.at[part], device_at(px, py, z_peers[i], core),
            ).start()

        return start

    for group in GROUPS:
        first, count = group[0], len(group)
        for i in group:
            if i == 7:
                own_left.wait()
                wait_bytes(right_all.at[pl.ds(0, 15), 0], left_recv.at[7])
            else:
                wait_bytes(left_all.at[:, 0], left_recv.at[i])
        left = jnp.concatenate(
            [rows_of(left_all[step, pl.ds(first, count)]) for step in range(4)], axis=1
        )
        for column in range(4):
            right = jnp.concatenate([rows_of(right_all[column * 4 + step]) for step in range(4)], axis=1)
            total = lax.dot_general(left, right, NT, preferred_element_type=F32)
            total = total.reshape(count, 4, 8, 128)
            for py in range(4):
                for part in range(2):
                    mixed_send[part, pl.ds(first, count), py * 4 + column] = total[
                        :, py, part * 4 : part * 4 + 4
                    ].astype(BF16)
        to_all(send_mixed(0), group)
    to_all(send_mixed(1), range(8))
    own_mixed = [own(mixed_send.at[part, 7, xy], mixed_all.at[part, z * 16 + xy], 2 + part) for part in range(2)]

    wait_bytes(edge_all.at[pl.ds(0, 3)], recv_sem.at[2])
    edge_sum = edge_all[0] + edge_all[1] + edge_all[2] + edge_all[3]
    out_gain = jnp.transpose(jnp.broadcast_to(edge_sum[0:1], (128, 128)))
    out_shift = jnp.transpose(jnp.broadcast_to(edge_sum[1:2], (128, 128)))

    own_out = []
    for part in range(2):
        own_mixed[part].wait()
        wait_bytes(mixed_all.at[part, pl.ds(0, 127)], mixed_recv.at[part])
        centred(mixed_all.at[part], wide)
        for step in range(2):
            normed = []
            for member in range(2):
                value = wide[pl.ds(step * 2 + member, 128, stride=4), :] * out_gain + out_shift
                normed.append(value.astype(BF16))
            projected = jnp.dot(
                w_out_t[...], jnp.concatenate(normed, axis=1), preferred_element_type=F32
            )
            for member in range(2):
                at = pl.ds((part * 4 + step * 2 + member) * 128, 128)
                left_f[at, :] = gate_f[at, :] * projected[:, member * 128 : member * 128 + 128]
        for t in (2, 1, 3, 0):
            ph = hi_peer(t)
            rows, place = out_send.at[part, pl.ds(ph * 2, 2)], out.at[:, :, z_hi, part]
            by_channel(left_f, out_send.at[part], ph * 2, 2, part * 512)
            if t:
                remote(rows, place, send_sem.at[8], out_sem.at[part], at_hi(ph)).start()
            else:
                own_out.append(own(rows, place, 4 + part))
    for part in range(2):
        own_out[part].wait()
        wait_bytes(out.at[:, :, pl.ds(0, 3), part], out_sem.at[part])

    wait_bytes(xin.at[pl.ds(0, 96)], send_sem.at[0])
    wait_bytes(w_all.at[pl.ds(3, 2), pl.ds(0, 3), pl.ds(0, 2)], send_sem.at[1])
    wait_bytes(edge_all.at[pl.ds(0, 3)], send_sem.at[2])
    wait_bytes(w_all.at[pl.ds(0, 3), :, pl.ds(0, 3)], send_sem.at[3])
    wait_bytes(w_all.at[pl.ds(3, 2), :, pl.ds(0, 2)], send_sem.at[4])
    wait_bytes(xin.at[pl.ds(0, 127)], send_sem.at[5])
    wait_bytes(xin.at[pl.ds(0, 127)], send_sem.at[6])
    wait_bytes(mixed_all.at[:, pl.ds(0, 127)], send_sem.at[7])
    wait_bytes(out.at[:, :, pl.ds(0, 3)], send_sem.at[8])
    wait_bytes(w_all.at[pl.ds(0, 3), pl.ds(0, 3), 0], send_sem.at[9])
    wait_bytes(right_all.at[:, pl.ds(0, 8)], sibling_send)


def on_device(
    pair,
    token_valid,
    ln_gain,
    ln_bias,
    w_agate,
    w_aproj,
    w_bgate,
    w_bproj,
    w_gate,
    out_gain,
    out_bias,
    w_out,
):
    any_spec = pl.BlockSpec(memory_space=pltpu.HBM)
    operands = [
        pltpu.with_memory_space_constraint(array, pltpu.HBM)
        for array in (
            pair.reshape(32, 4, 8, 128),
            token_valid.reshape(4, 128),
            token_valid,
            ln_gain,
            ln_bias,
            w_agate.T.reshape(4, 8, 128),
            w_aproj.T.reshape(4, 8, 128),
            w_gate.T.reshape(4, 8, 128),
            w_bgate.T.reshape(4, 8, 128),
            w_bproj.T.reshape(4, 8, 128),
            out_gain,
            out_bias,
            w_out,
        )
    ]
    result = pl.pallas_call(
        kernel,
        name="triangle",
        out_shape=pltpu.VMEM((2, 16, 4, 2, 4, 128), BF16),
        in_specs=[any_spec] * 13,
        out_specs=pl.BlockSpec(memory_space=pl.ANY),
        scratch_shapes=[
            pltpu.VMEM((128, 8, 128), BF16),
            pltpu.VMEM((4, 128), jnp.int32),
            pltpu.SMEM((512,), jnp.int32),
            pltpu.SMEM((128,), F32),
            pltpu.SMEM((128,), F32),
            pltpu.SMEM((32,), F32),
            pltpu.SMEM((32,), F32),
                pltpu.VMEM((128, 128), BF16),
            pltpu.VMEM((5, 4, 4, 8, 128), BF16),
            pltpu.VMEM((128, 128), BF16),
            pltpu.VMEM((8, 128), F32),
            pltpu.VMEM((4, 8, 128), F32),
            pltpu.VMEM((1024, 128), F32),
            pltpu.VMEM((1024, 128), F32),
            pltpu.VMEM((1024, 128), F32),
            pltpu.VMEM((1024, 128), F32),
            pltpu.VMEM((8, 16, 8, 128), BF16),
            pltpu.VMEM((4, 8, 4, 8, 128), BF16),
            pltpu.VMEM((8, 16, 8, 128), BF16),
            pltpu.VMEM((16, 16, 8, 128), BF16),
            pltpu.VMEM((2, 8, 16, 4, 128), BF16),
            pltpu.VMEM((2, 128, 4, 128), BF16),
            pltpu.VMEM((2, 8, 16, 4, 128), BF16),
            pltpu.SemaphoreType.DMA((13,)),
            pltpu.SemaphoreType.DMA((10,)),
            pltpu.SemaphoreType.DMA((10,)),
            pltpu.SemaphoreType.DMA((6,)),
            pltpu.SemaphoreType.DMA,
            pltpu.SemaphoreType.DMA((8,)),
            pltpu.SemaphoreType.DMA((8,)),
            pltpu.SemaphoreType.DMA,
            pltpu.SemaphoreType.DMA((2,)),
            pltpu.SemaphoreType.DMA((2,)),
            pltpu.SemaphoreType.REGULAR,
        ],
        compiler_params=pltpu.CompilerParams(
            collective_id=0, has_side_effects=True, vmem_limit_bytes=32 << 20
        ),
    )(*operands)
    return result.reshape(32, 32, 128)


def solution(mesh):
    return jax.shard_map(
        on_device,
        mesh=mesh,
        in_specs=(
            P("chan", "row", "col"),
            P(),
            P(),
            P(),
            P(None, "chan"),
            P(None, "chan"),
            P(None, "chan"),
            P(None, "chan"),
            P(None, "chan"),
            P("chan"),
            P("chan"),
            P(),
        ),
        out_specs=P("chan", "row", "col"),
        check_vma=False,
    )
```

```python
import jax
import jax.numpy as jnp
from jax import lax
from jax.experimental import pallas as pl
from jax.experimental.pallas import tpu as pltpu
from jax.sharding import PartitionSpec as P

EPSILON = 1e-05
MESH = pl.DeviceIdType.MESH
F32 = jnp.float32
BF16 = jnp.bfloat16
NT = (((1,), (1,)), ((), ()))
Z_AWAY = (4, 3, 5, 2, 6, 1, 7, 0)
MIRROR = (0, 2, 1, 4, 3, 6, 5, 7)
GROUPS = ((0, 1, 2), (3, 4), (5, 6, 7))


def device_at(x, y, z, core):
    return ((y * 2 + z % 2) * 2 + core, x, z // 2)


def wait_bytes(ref, sem):
    pltpu.make_async_copy(ref, ref, sem).wait()


def remote(src, dst, send_sem, recv_sem, device):
    return pltpu.make_async_remote_copy(
        src, dst, send_sem, recv_sem, device_id=device, device_id_type=MESH
    )


def rows_of(block):
    return block.astype(F32).reshape(-1, 128).astype(BF16)


def one_hot(shape, offset):
    first = lax.broadcasted_iota(jnp.int32, shape, 0)
    second = lax.broadcasted_iota(jnp.int32, shape, 1)
    return (second == first + offset).astype(F32).astype(BF16)


def centred(blocks, scratch, gain=None, shift=None):
    n = blocks.shape[1]

    def add(step, total):
        part = blocks[pl.ds(step * 16, 16)].astype(F32)
        return total + jnp.sum(part, axis=0)

    centre = lax.fori_loop(0, 8, add, jnp.zeros((n, 128), F32)) * (1.0 / 128)

    def add_square(step, total):
        part = blocks[pl.ds(step * 16, 16)].astype(F32) - centre
        return total + jnp.sum(part * part, axis=0)

    spread = lax.fori_loop(0, 8, add_square, jnp.zeros((n, 128), F32)) * (1.0 / 128)
    scale = lax.rsqrt(spread + EPSILON)

    def put(step, _):
        for member in range(16):
            c = step * 16 + member
            value = (blocks[c].astype(F32) - centre) * scale
            if gain is not None:
                value = value * gain[c] + shift[c]
            scratch[pl.ds(pl.multiple_of(c * n, n), n), :] = value
        return 0

    lax.fori_loop(0, 8, put, 0)


def by_channel(scratch, out, first=0, count=8, base=0):
    n = out.shape[2]

    def put(step, _):
        for member in range(16):
            out[step, member] = scratch[pl.ds(base + step * 16 + member, n, stride=128), :].astype(BF16)
        return 0

    lax.fori_loop(first, first + count, put, 0)


def kernel(
    pair, valid_row, valid_s_in, gain_in, bias_in, w0, w1, w2, w3, w4, out_gain_in, out_bias_in, w_out_in,
    out,
    xin, valid_v, valid_s, gain_s, bias_s, out_gain_s, out_bias_s, w_out_v, w_all, w_out_t,
    edge, edge_all,
    wide, left_f, right_f, gate_f,
    left_send, left_all, right_send, right_all, mixed_send, mixed_all, out_send,
    load_sem, send_sem, recv_sem, own_sem, sibling_send, left_recv, right_recv, sibling_recv, mixed_recv, out_sem, plane_sem,
):
    row, x, z_hi = lax.axis_index("row"), lax.axis_index("col"), lax.axis_index("chan")
    core, z_lo, y = row % 2, (row // 2) % 2, row // 4
    z = z_hi * 2 + z_lo
    xy = y * 4 + x

    def hi_peer(t):
        return (z_hi + t + core * (4 - 2 * t)) % 4

    def at_hi(ph):
        return (row, x, ph)

    sibling = device_at(x, y, z, 1 - core)
    z_peers = [(z + away + core * (8 - 2 * away)) % 8 for away in Z_AWAY]

    barrier = pltpu.get_barrier_semaphore()
    for pz in z_peers[:7]:
        pl.semaphore_signal(
            barrier, inc=1, device_id=device_at(x, y, pz, core), device_id_type=MESH
        )

    def greet_xy(t, _):
        pl.semaphore_signal(
            barrier,
            inc=1,
            device_id=device_at((x + t % 4) % 4, (y + t // 4) % 4, z, core),
            device_id_type=MESH,
        )
        return 0

    lax.fori_loop(1, 16, greet_xy, 0)
    pl.semaphore_signal(barrier, inc=1, device_id=sibling, device_id_type=MESH)

    own_rows = pltpu.make_async_copy(pair.at[:, z_hi], xin.at[pl.ds(z_hi * 32, 32)], load_sem.at[0])
    weight_loads = [
        pltpu.make_async_copy(w.at[x], w_all.at[t, z_hi, x], load_sem.at[1 + t])
        for t, w in enumerate((w0, w1, w2, w3, w4))
    ]
    out_loads = [
        pltpu.make_async_copy(w_out_in, w_out_v, load_sem.at[6]),
        pltpu.make_async_copy(out_gain_in, out_gain_s, load_sem.at[7]),
        pltpu.make_async_copy(out_bias_in, out_bias_s, load_sem.at[8]),
    ]
    in_loads = [
        pltpu.make_async_copy(valid_row, valid_v, load_sem.at[9]),
        pltpu.make_async_copy(valid_s_in, valid_s, load_sem.at[10]),
        pltpu.make_async_copy(gain_in, gain_s, load_sem.at[11]),
        pltpu.make_async_copy(bias_in, bias_s, load_sem.at[12]),
    ]
    for copy in weight_loads + out_loads + in_loads + [own_rows]:
        copy.start()
    for copy in weight_loads + out_loads:
        copy.wait()
    lane = lax.broadcasted_iota(jnp.int32, (8, 128), 1)
    line = lax.broadcasted_iota(jnp.int32, (8, 128), 0)

    def put_edge(i, held):
        value = jnp.where(line == 0, out_gain_s[i], out_bias_s[i])
        return jnp.where(lane == z_hi * 32 + i, value, held)

    edge[...] = lax.fori_loop(0, 32, put_edge, jnp.zeros((8, 128), F32))
    edge_all[z_hi] = edge[...]
    w_out_t[...] = lax.dot_general(
        one_hot((128, 128), 0), w_out_v[...], NT, preferred_element_type=F32
    ).astype(BF16)

    pl.semaphore_wait(barrier, 23)

    left_weights = w_all.at[:, z_hi, x]
    for t in (2, 1, 3):
        ph = hi_peer(t)
        remote(left_weights, left_weights, send_sem.at[9], recv_sem.at[9], at_hi(ph)).start()
    for t in (2, 1, 3):
        ph = hi_peer(t)
        remote(
            pair.at[:, ph], xin.at[pl.ds(z_hi * 32, 32)], send_sem.at[0], recv_sem.at[0], at_hi(ph)
        ).start()
    for pz in z_peers[:7]:
        pl.semaphore_signal(
            plane_sem, inc=1, device_id=device_at(x, y, pz, core), device_id_type=MESH
        )
    for t in (2, 1, 3):
        ph = hi_peer(t)
        remote(edge, edge_all.at[z_hi], send_sem.at[2], recv_sem.at[2], at_hi(ph)).start()
    for copy in in_loads:
        copy.wait()
    wait_bytes(w_all.at[:, pl.ds(0, 3), 0], recv_sem.at[9])
    left_weights = w_all.at[:, :, x]
    for t in (2, 1, 3):
        remote(
            left_weights, left_weights, send_sem.at[3], recv_sem.at[3],
            device_at((x + t) % 4, y, z, core),
        ).start()

    own_rows.wait()
    wait_bytes(xin.at[pl.ds(0, 96)], recv_sem.at[0])
    centred(xin, wide, gain_s, bias_s)

    wait_bytes(w_all.at[:, :, pl.ds(0, 3)], recv_sem.at[3])
    col_valid = valid_v[pl.ds(x, 1), :].astype(F32)
    first_row = row * 32 + z_hi * 8

    def rows_at(step):
        normed = [wide[pl.ds(step * 2 + member, 128, stride=8), :].astype(BF16) for member in range(2)]
        return jnp.concatenate(normed, axis=1)

    def linear(t, normed):
        return jnp.dot(rows_of(w_all[t]), normed, preferred_element_type=F32)

    def put_rows(ref, step, value):
        for member in range(2):
            at = pl.ds(pl.multiple_of((step * 2 + member) * 128, 128), 128)
            ref[at, :] = value[:, member * 128 : member * 128 + 128]

    def edges(first, ref):
        def project(step, _):
            normed = rows_at(step)
            masks = [
                col_valid * valid_s[first_row + step * 2 + member].astype(F32) for member in range(2)
            ]
            value = jax.nn.sigmoid(linear(first, normed)) * linear(first + 1, normed)
            put_rows(ref, step, value * jnp.concatenate(masks, axis=1))
            return 0

        lax.fori_loop(0, 4, project, 0, unroll=True)

    def gates(step, _):
        value = jax.nn.sigmoid(linear(2, rows_at(step)))
        put_rows(gate_f, step, value.astype(BF16).astype(F32))
        return 0

    def own(src, dst, i):
        copy = pltpu.make_async_copy(src, dst, own_sem.at[i])
        copy.start()
        return copy

    def to_all(start, places, prepare=None):
        for i in places:
            if prepare is not None:
                prepare(z_peers[i])

            def line(j, _):
                py = (y + 2 + j + core * (4 - 2 * j)) % 4
                for m in range(4):
                    px = (x + 2 + m + core * (4 - 2 * m)) % 4
                    if i < 7 or m != 2:
                        start(i, px, py, py * 4 + px)
                    else:
                        pl.when(j != 2)(lambda: start(i, px, py, py * 4 + px))
                return 0

            lax.fori_loop(0, 4, line, 0)

    edges(3, right_f)
    pl.semaphore_wait(plane_sem, 7)

    def slot(pz, pcore):
        return (pz % 2) * 8 + pcore * 4 + pz // 2

    mine = slot(z, core)

    def send_right(i, px, py, pxy):
        remote(
            right_send.at[z_peers[i], pxy], right_all.at[xy, mine],
            send_sem.at[5], right_recv.at[MIRROR[i]], device_at(px, py, z_peers[i], core),
        ).start()

    to_all(send_right, range(8), lambda pz: by_channel(right_f, right_send, pz, 1))
    own_right = own(right_send.at[z, xy], right_all.at[xy, mine], 0)

    edges(0, left_f)

    def send_left(i, px, py, pxy):
        remote(
            left_send.at[z_peers[i], pxy], left_all.at[x, MIRROR[i], y],
            send_sem.at[6], left_recv.at[MIRROR[i]], device_at(px, py, z_peers[i], core),
        ).start()

    to_all(send_left, range(8), lambda pz: by_channel(left_f, left_send, pz, 1))
    own_left = own(left_send.at[z, xy], left_all.at[x, 7, y], 1)
    lax.fori_loop(0, 4, gates, 0, unroll=True)

    for i in range(8):
        if i == 7:
            own_right.wait()
            wait_bytes(right_all.at[pl.ds(0, 15), 0], right_recv.at[7])
        else:
            wait_bytes(right_all.at[:, 0], right_recv.at[i])
        part = right_all.at[:, slot(z_peers[i], core)]
        remote(part, part, sibling_send, sibling_recv, sibling).start()
    wait_bytes(right_all.at[:, pl.ds(0, 8)], sibling_recv)

    def send_mixed(part):
        def start(i, px, py, pxy):
            remote(
                mixed_send.at[part, i, pxy], mixed_all.at[part, z * 16 + xy],
                send_sem.at[7], mixed_recv.at[part], device_at(px, py, z_peers[i], core),
            ).start()

        return start

    for group in GROUPS:
        first, count = group[0], len(group)
        for i in group:
            if i == 7:
                own_left.wait()
                wait_bytes(right_all.at[pl.ds(0, 15), 0], left_recv.at[7])
            else:
                wait_bytes(left_all.at[:, 0], left_recv.at[i])
        left = jnp.concatenate(
            [rows_of(left_all[step, pl.ds(first, count)]) for step in range(4)], axis=1
        )
        for column in range(4):
            right = jnp.concatenate([rows_of(right_all[column * 4 + step]) for step in range(4)], axis=1)
            total = lax.dot_general(left, right, NT, preferred_element_type=F32)
            total = total.reshape(count, 4, 8, 128)
            for py in range(4):
                for part in range(2):
                    mixed_send[part, pl.ds(first, count), py * 4 + column] = total[
                        :, py, part * 4 : part * 4 + 4
                    ].astype(BF16)
        to_all(send_mixed(0), group)
    to_all(send_mixed(1), range(8))
    own_mixed = [own(mixed_send.at[part, 7, xy], mixed_all.at[part, z * 16 + xy], 2 + part) for part in range(2)]

    wait_bytes(edge_all.at[pl.ds(0, 3)], recv_sem.at[2])
    edge_sum = edge_all[0] + edge_all[1] + edge_all[2] + edge_all[3]
    out_gain = jnp.transpose(jnp.broadcast_to(edge_sum[0:1], (128, 128)))
    out_shift = jnp.transpose(jnp.broadcast_to(edge_sum[1:2], (128, 128)))

    own_out = []
    for part in range(2):
        own_mixed[part].wait()
        wait_bytes(mixed_all.at[part, pl.ds(0, 127)], mixed_recv.at[part])
        centred(mixed_all.at[part], wide)
        for step in range(2):
            normed = []
            for member in range(2):
                value = wide[pl.ds(step * 2 + member, 128, stride=4), :] * out_gain + out_shift
                normed.append(value.astype(BF16))
            projected = jnp.dot(
                w_out_t[...], jnp.concatenate(normed, axis=1), preferred_element_type=F32
            )
            for member in range(2):
                at = pl.ds((part * 4 + step * 2 + member) * 128, 128)
                left_f[at, :] = gate_f[at, :] * projected[:, member * 128 : member * 128 + 128]
        for t in (2, 1, 3, 0):
            ph = hi_peer(t)
            rows, place = out_send.at[part, pl.ds(ph * 2, 2)], out.at[:, :, z_hi, part]
            by_channel(left_f, out_send.at[part], ph * 2, 2, part * 512)
            if t:
                remote(rows, place, send_sem.at[8], out_sem.at[part], at_hi(ph)).start()
            else:
                own_out.append(own(rows, place, 4 + part))
    for part in range(2):
        own_out[part].wait()
        wait_bytes(out.at[:, :, pl.ds(0, 3), part], out_sem.at[part])

    wait_bytes(xin.at[pl.ds(0, 96)], send_sem.at[0])
    wait_bytes(edge_all.at[pl.ds(0, 3)], send_sem.at[2])
    wait_bytes(w_all.at[:, :, pl.ds(0, 3)], send_sem.at[3])
    wait_bytes(xin.at[pl.ds(0, 127)], send_sem.at[5])
    wait_bytes(xin.at[pl.ds(0, 127)], send_sem.at[6])
    wait_bytes(mixed_all.at[:, pl.ds(0, 127)], send_sem.at[7])
    wait_bytes(out.at[:, :, pl.ds(0, 3)], send_sem.at[8])
    wait_bytes(w_all.at[:, pl.ds(0, 3), 0], send_sem.at[9])
    wait_bytes(right_all.at[:, pl.ds(0, 8)], sibling_send)


def on_device(
    pair,
    token_valid,
    ln_gain,
    ln_bias,
    w_agate,
    w_aproj,
    w_bgate,
    w_bproj,
    w_gate,
    out_gain,
    out_bias,
    w_out,
):
    any_spec = pl.BlockSpec(memory_space=pltpu.HBM)
    operands = [
        pltpu.with_memory_space_constraint(array, pltpu.HBM)
        for array in (
            pair.reshape(32, 4, 8, 128),
            token_valid.reshape(4, 128),
            token_valid,
            ln_gain,
            ln_bias,
            w_agate.T.reshape(4, 8, 128),
            w_aproj.T.reshape(4, 8, 128),
            w_gate.T.reshape(4, 8, 128),
            w_bgate.T.reshape(4, 8, 128),
            w_bproj.T.reshape(4, 8, 128),
            out_gain,
            out_bias,
            w_out,
        )
    ]
    result = pl.pallas_call(
        kernel,
        name="triangle",
        out_shape=pltpu.VMEM((2, 16, 4, 2, 4, 128), BF16),
        in_specs=[any_spec] * 13,
        out_specs=pl.BlockSpec(memory_space=pl.ANY),
        scratch_shapes=[
            pltpu.VMEM((128, 8, 128), BF16),
            pltpu.VMEM((4, 128), jnp.int32),
            pltpu.SMEM((512,), jnp.int32),
            pltpu.SMEM((128,), F32),
            pltpu.SMEM((128,), F32),
            pltpu.SMEM((32,), F32),
            pltpu.SMEM((32,), F32),
                pltpu.VMEM((128, 128), BF16),
            pltpu.VMEM((5, 4, 4, 8, 128), BF16),
            pltpu.VMEM((128, 128), BF16),
            pltpu.VMEM((8, 128), F32),
            pltpu.VMEM((4, 8, 128), F32),
            pltpu.VMEM((1024, 128), F32),
            pltpu.VMEM((1024, 128), F32),
            pltpu.VMEM((1024, 128), F32),
            pltpu.VMEM((1024, 128), F32),
            pltpu.VMEM((8, 16, 8, 128), BF16),
            pltpu.VMEM((4, 8, 4, 8, 128), BF16),
            pltpu.VMEM((8, 16, 8, 128), BF16),
            pltpu.VMEM((16, 16, 8, 128), BF16),
            pltpu.VMEM((2, 8, 16, 4, 128), BF16),
            pltpu.VMEM((2, 128, 4, 128), BF16),
            pltpu.VMEM((2, 8, 16, 4, 128), BF16),
            pltpu.SemaphoreType.DMA((13,)),
            pltpu.SemaphoreType.DMA((10,)),
            pltpu.SemaphoreType.DMA((10,)),
            pltpu.SemaphoreType.DMA((6,)),
            pltpu.SemaphoreType.DMA,
            pltpu.SemaphoreType.DMA((8,)),
            pltpu.SemaphoreType.DMA((8,)),
            pltpu.SemaphoreType.DMA,
            pltpu.SemaphoreType.DMA((2,)),
            pltpu.SemaphoreType.DMA((2,)),
            pltpu.SemaphoreType.REGULAR,
        ],
        compiler_params=pltpu.CompilerParams(
            collective_id=0, has_side_effects=True, vmem_limit_bytes=32 << 20
        ),
    )(*operands)
    return result.reshape(32, 32, 128)


def solution(mesh):
    return jax.shard_map(
        on_device,
        mesh=mesh,
        in_specs=(
            P("chan", "row", "col"),
            P(),
            P(),
            P(),
            P(None, "chan"),
            P(None, "chan"),
            P(None, "chan"),
            P(None, "chan"),
            P(None, "chan"),
            P("chan"),
            P("chan"),
            P(),
        ),
        out_specs=P("chan", "row", "col"),
        check_vma=False,
    )
```

```python
import jax
import jax.numpy as jnp
from jax import lax
from jax.experimental import pallas as pl
from jax.experimental.pallas import tpu as pltpu
from jax.sharding import PartitionSpec as P

EPSILON = 1e-05
MESH = pl.DeviceIdType.MESH
F32 = jnp.float32
BF16 = jnp.bfloat16
NT = (((1,), (1,)), ((), ()))
Z_AWAY = (4, 3, 5, 2, 6, 1, 7, 0)
MIRROR = (0, 2, 1, 4, 3, 6, 5, 7)
GROUPS = ((0, 1, 2), (3, 4), (5, 6, 7))


def device_at(x, y, z, core):
    return ((y * 2 + z % 2) * 2 + core, x, z // 2)


def wait_bytes(ref, sem):
    pltpu.make_async_copy(ref, ref, sem).wait()


def remote(src, dst, send_sem, recv_sem, device):
    return pltpu.make_async_remote_copy(
        src, dst, send_sem, recv_sem, device_id=device, device_id_type=MESH
    )


def rows_of(block):
    return block.astype(F32).reshape(-1, 128).astype(BF16)


def one_hot(shape, offset):
    first = lax.broadcasted_iota(jnp.int32, shape, 0)
    second = lax.broadcasted_iota(jnp.int32, shape, 1)
    return (second == first + offset).astype(F32).astype(BF16)


def sums(blocks, shift, first, count):
    def add(step, totals):
        part = blocks[pl.ds(first + step * 16, 16)].astype(F32) - shift
        return totals[0] + jnp.sum(part, axis=0), totals[1] + jnp.sum(part * part, axis=0)

    zero = jnp.zeros(blocks.shape[1:], F32)
    return lax.fori_loop(0, count // 16, add, (zero, zero))


def centred(blocks, scratch, total, square, shift, gain=None, offset=None):
    n = blocks.shape[1]
    above = total * (1.0 / 128)
    spread = square * (1.0 / 128) - above * above
    centre, scale = shift + above, lax.rsqrt(spread + EPSILON)

    def put(step, _):
        for member in range(16):
            c = step * 16 + member
            value = (blocks[c].astype(F32) - centre) * scale
            if gain is not None:
                value = value * gain[c] + offset[c]
            scratch[pl.ds(pl.multiple_of(c * n, n), n), :] = value
        return 0

    lax.fori_loop(0, 8, put, 0)


def by_channel(scratch, out, first=0, count=8, base=0):
    n = out.shape[2]

    def put(step, _):
        for member in range(16):
            out[step, member] = scratch[pl.ds(base + step * 16 + member, n, stride=128), :].astype(BF16)
        return 0

    lax.fori_loop(first, first + count, put, 0)


def kernel(
    pair, valid_row, valid_s_in, gain_in, bias_in, w0, w1, w2, w3, w4, out_gain_in, out_bias_in, w_out_in,
    out,
    xin, valid_v, valid_s, gain_s, bias_s, out_gain_s, out_bias_s, w_out_v, w_all, w_out_t,
    edge, edge_all,
    wide, left_f, right_f, gate_f,
    left_send, left_all, right_send, right_all, mixed_send, mixed_all, out_send,
    load_sem, send_sem, recv_sem, own_sem, sibling_send, left_recv, right_recv, sibling_recv, xin_sem, mixed_recv, out_sem, plane_sem,
):
    row, x, z_hi = lax.axis_index("row"), lax.axis_index("col"), lax.axis_index("chan")
    core, z_lo, y = row % 2, (row // 2) % 2, row // 4
    z = z_hi * 2 + z_lo
    xy = y * 4 + x

    def hi_peer(t):
        return (z_hi + t + core * (4 - 2 * t)) % 4

    def at_hi(ph):
        return (row, x, ph)

    sibling = device_at(x, y, z, 1 - core)
    z_peers = [(z + away + core * (8 - 2 * away)) % 8 for away in Z_AWAY]

    barrier = pltpu.get_barrier_semaphore()
    for pz in z_peers[:7]:
        pl.semaphore_signal(
            barrier, inc=1, device_id=device_at(x, y, pz, core), device_id_type=MESH
        )

    def greet_xy(t, _):
        pl.semaphore_signal(
            barrier,
            inc=1,
            device_id=device_at((x + t % 4) % 4, (y + t // 4) % 4, z, core),
            device_id_type=MESH,
        )
        return 0

    lax.fori_loop(1, 16, greet_xy, 0)
    pl.semaphore_signal(barrier, inc=1, device_id=sibling, device_id_type=MESH)

    own_rows = pltpu.make_async_copy(pair.at[:, z_hi], xin.at[pl.ds(z_hi * 32, 32)], load_sem.at[0])
    weight_loads = [
        pltpu.make_async_copy(w.at[x], w_all.at[t, z_hi, x], load_sem.at[1 + t])
        for t, w in enumerate((w0, w1, w2, w3, w4))
    ]
    out_loads = [
        pltpu.make_async_copy(w_out_in, w_out_v, load_sem.at[6]),
        pltpu.make_async_copy(out_gain_in, out_gain_s, load_sem.at[7]),
        pltpu.make_async_copy(out_bias_in, out_bias_s, load_sem.at[8]),
    ]
    in_loads = [
        pltpu.make_async_copy(valid_row, valid_v, load_sem.at[9]),
        pltpu.make_async_copy(valid_s_in, valid_s, load_sem.at[10]),
        pltpu.make_async_copy(gain_in, gain_s, load_sem.at[11]),
        pltpu.make_async_copy(bias_in, bias_s, load_sem.at[12]),
    ]
    for copy in weight_loads + out_loads + in_loads + [own_rows]:
        copy.start()
    for copy in weight_loads + out_loads:
        copy.wait()
    lane = lax.broadcasted_iota(jnp.int32, (8, 128), 1)
    line = lax.broadcasted_iota(jnp.int32, (8, 128), 0)

    def put_edge(i, held):
        value = jnp.where(line == 0, out_gain_s[i], out_bias_s[i])
        return jnp.where(lane == z_hi * 32 + i, value, held)

    edge[...] = lax.fori_loop(0, 32, put_edge, jnp.zeros((8, 128), F32))
    edge_all[z_hi] = edge[...]
    w_out_t[...] = lax.dot_general(
        one_hot((128, 128), 0), w_out_v[...], NT, preferred_element_type=F32
    ).astype(BF16)

    pl.semaphore_wait(barrier, 23)

    left_weights = w_all.at[:, z_hi, x]
    for t in (2, 1, 3):
        ph = hi_peer(t)
        remote(left_weights, left_weights, send_sem.at[9], recv_sem.at[9], at_hi(ph)).start()
    for t in (2, 1, 3):
        ph = hi_peer(t)
        remote(
            pair.at[:, ph], xin.at[pl.ds(z_hi * 32, 32)], send_sem.at[0], xin_sem.at[t], at_hi(ph)
        ).start()
    for pz in z_peers[:7]:
        pl.semaphore_signal(
            plane_sem, inc=1, device_id=device_at(x, y, pz, core), device_id_type=MESH
        )
    for copy in in_loads:
        copy.wait()
    wait_bytes(w_all.at[:, pl.ds(0, 3), 0], recv_sem.at[9])
    left_weights = w_all.at[:, :, x]
    for t in (2, 1, 3):
        remote(
            left_weights, left_weights, send_sem.at[3], recv_sem.at[3],
            device_at((x + t) % 4, y, z, core),
        ).start()

    own_rows.wait()
    own_total, _ = sums(xin, 0.0, z_hi * 32, 32)
    shift = own_total * (1.0 / 32)
    total, square = sums(xin, shift, z_hi * 32, 32)
    for t in (1, 3, 2):
        wait_bytes(xin.at[pl.ds(0, 32)], xin_sem.at[t])
        more = sums(xin, shift, hi_peer(4 - t) * 32, 32)
        total, square = total + more[0], square + more[1]
    centred(xin, wide, total, square, shift, gain_s, bias_s)

    wait_bytes(w_all.at[:, :, pl.ds(0, 3)], recv_sem.at[3])
    col_valid = valid_v[pl.ds(x, 1), :].astype(F32)
    first_row = row * 32 + z_hi * 8

    def rows_at(step):
        normed = [wide[pl.ds(step * 2 + member, 128, stride=8), :].astype(BF16) for member in range(2)]
        return jnp.concatenate(normed, axis=1)

    def linear(weight, normed):
        return jnp.dot(weight, normed, preferred_element_type=F32)

    def put_rows(ref, step, value):
        for member in range(2):
            at = pl.ds(pl.multiple_of((step * 2 + member) * 128, 128), 128)
            ref[at, :] = value[:, member * 128 : member * 128 + 128]

    def edges(first, ref):
        gate_rows, value_rows = rows_of(w_all[first]), rows_of(w_all[first + 1])

        def project(step, _):
            normed = rows_at(step)
            masks = [
                col_valid * valid_s[first_row + step * 2 + member].astype(F32) for member in range(2)
            ]
            value = jax.nn.sigmoid(linear(gate_rows, normed)) * linear(value_rows, normed)
            put_rows(ref, step, value * jnp.concatenate(masks, axis=1))
            return 0

        lax.fori_loop(0, 4, project, 0, unroll=True)

    def gates(step, _):
        value = jax.nn.sigmoid(linear(rows_of(w_all[2]), rows_at(step)))
        put_rows(gate_f, step, value.astype(BF16).astype(F32))
        return 0

    def own(src, dst, i):
        copy = pltpu.make_async_copy(src, dst, own_sem.at[i])
        copy.start()
        return copy

    def to_all(start, places, prepare=None):
        for i in places:
            if prepare is not None:
                prepare(z_peers[i])

            def line(j, _):
                py = (y + 2 + j + core * (4 - 2 * j)) % 4
                for m in range(4):
                    px = (x + 2 + m + core * (4 - 2 * m)) % 4
                    if i < 7 or m != 2:
                        start(i, px, py, py * 4 + px)
                    else:
                        pl.when(j != 2)(lambda: start(i, px, py, py * 4 + px))
                return 0

            lax.fori_loop(0, 4, line, 0)

    edges(3, right_f)
    pl.semaphore_wait(plane_sem, 7)

    def slot(pz, pcore):
        return (pz % 2) * 8 + pcore * 4 + pz // 2

    mine = slot(z, core)

    def send_right(i, px, py, pxy):
        remote(
            right_send.at[z_peers[i], pxy], right_all.at[xy, mine],
            send_sem.at[5], right_recv.at[MIRROR[i]], device_at(px, py, z_peers[i], core),
        ).start()

    to_all(send_right, range(8), lambda pz: by_channel(right_f, right_send, pz, 1))
    own_right = own(right_send.at[z, xy], right_all.at[xy, mine], 0)

    edges(0, left_f)

    def send_left(i, px, py, pxy):
        remote(
            left_send.at[z_peers[i], pxy], left_all.at[x, MIRROR[i], y],
            send_sem.at[6], left_recv.at[MIRROR[i]], device_at(px, py, z_peers[i], core),
        ).start()

    to_all(send_left, range(8), lambda pz: by_channel(left_f, left_send, pz, 1))
    own_left = own(left_send.at[z, xy], left_all.at[x, 7, y], 1)
    for t in (2, 1, 3):
        ph = hi_peer(t)
        remote(edge, edge_all.at[z_hi], send_sem.at[2], recv_sem.at[2], at_hi(ph)).start()
    lax.fori_loop(0, 4, gates, 0, unroll=True)

    for i in range(8):
        if i == 7:
            own_right.wait()
            wait_bytes(right_all.at[pl.ds(0, 15), 0], right_recv.at[7])
        else:
            wait_bytes(right_all.at[:, 0], right_recv.at[i])
        part = right_all.at[:, slot(z_peers[i], core)]
        remote(part, part, sibling_send, sibling_recv, sibling).start()
    wait_bytes(right_all.at[:, pl.ds(0, 8)], sibling_recv)

    def send_mixed(part):
        def start(i, px, py, pxy):
            remote(
                mixed_send.at[part, i, pxy], mixed_all.at[part, z * 16 + xy],
                send_sem.at[7], mixed_recv.at[part], device_at(px, py, z_peers[i], core),
            ).start()

        return start

    for group in GROUPS:
        first, count = group[0], len(group)
        for i in group:
            if i == 7:
                own_left.wait()
                wait_bytes(right_all.at[pl.ds(0, 15), 0], left_recv.at[7])
            else:
                wait_bytes(left_all.at[:, 0], left_recv.at[i])
        left = jnp.concatenate(
            [rows_of(left_all[step, pl.ds(first, count)]) for step in range(4)], axis=1
        )
        for column in range(4):
            right = jnp.concatenate([rows_of(right_all[column * 4 + step]) for step in range(4)], axis=1)
            total = lax.dot_general(left, right, NT, preferred_element_type=F32)
            total = total.reshape(count, 4, 8, 128)
            for py in range(4):
                for part in range(2):
                    mixed_send[part, pl.ds(first, count), py * 4 + column] = total[
                        :, py, part * 4 : part * 4 + 4
                    ].astype(BF16)
        to_all(send_mixed(0), group)
    to_all(send_mixed(1), range(8))
    own_mixed = [own(mixed_send.at[part, 7, xy], mixed_all.at[part, z * 16 + xy], 2 + part) for part in range(2)]

    wait_bytes(edge_all.at[pl.ds(0, 3)], recv_sem.at[2])
    edge_sum = edge_all[0] + edge_all[1] + edge_all[2] + edge_all[3]
    out_gain = jnp.transpose(jnp.broadcast_to(edge_sum[0:1], (128, 128)))
    out_shift = jnp.transpose(jnp.broadcast_to(edge_sum[1:2], (128, 128)))

    own_out = []
    for part in range(2):
        own_mixed[part].wait()
        wait_bytes(mixed_all.at[part, pl.ds(0, 127)], mixed_recv.at[part])
        centred(mixed_all.at[part], wide, *sums(mixed_all.at[part], 0.0, 0, 128), 0.0)
        for step in range(2):
            normed = []
            for member in range(2):
                value = wide[pl.ds(step * 2 + member, 128, stride=4), :] * out_gain + out_shift
                normed.append(value.astype(BF16))
            projected = jnp.dot(
                w_out_t[...], jnp.concatenate(normed, axis=1), preferred_element_type=F32
            )
            for member in range(2):
                at = pl.ds((part * 4 + step * 2 + member) * 128, 128)
                left_f[at, :] = gate_f[at, :] * projected[:, member * 128 : member * 128 + 128]
        for t in (2, 1, 3, 0):
            ph = hi_peer(t)
            rows, place = out_send.at[part, pl.ds(ph * 2, 2)], out.at[:, :, z_hi, part]
            by_channel(left_f, out_send.at[part], ph * 2, 2, part * 512)
            if t:
                remote(rows, place, send_sem.at[8], out_sem.at[part], at_hi(ph)).start()
            else:
                own_out.append(own(rows, place, 4 + part))
    for part in range(2):
        own_out[part].wait()
        wait_bytes(out.at[:, :, pl.ds(0, 3), part], out_sem.at[part])

    wait_bytes(xin.at[pl.ds(0, 96)], send_sem.at[0])
    wait_bytes(edge_all.at[pl.ds(0, 3)], send_sem.at[2])
    wait_bytes(w_all.at[:, :, pl.ds(0, 3)], send_sem.at[3])
    wait_bytes(xin.at[pl.ds(0, 127)], send_sem.at[5])
    wait_bytes(xin.at[pl.ds(0, 127)], send_sem.at[6])
    wait_bytes(mixed_all.at[:, pl.ds(0, 127)], send_sem.at[7])
    wait_bytes(out.at[:, :, pl.ds(0, 3)], send_sem.at[8])
    wait_bytes(w_all.at[:, pl.ds(0, 3), 0], send_sem.at[9])
    wait_bytes(right_all.at[:, pl.ds(0, 8)], sibling_send)


def on_device(
    pair,
    token_valid,
    ln_gain,
    ln_bias,
    w_agate,
    w_aproj,
    w_bgate,
    w_bproj,
    w_gate,
    out_gain,
    out_bias,
    w_out,
):
    any_spec = pl.BlockSpec(memory_space=pltpu.HBM)
    operands = [
        pltpu.with_memory_space_constraint(array, pltpu.HBM)
        for array in (
            pair.reshape(32, 4, 8, 128),
            token_valid.reshape(4, 128),
            token_valid,
            ln_gain,
            ln_bias,
            w_agate.T.reshape(4, 8, 128),
            w_aproj.T.reshape(4, 8, 128),
            w_gate.T.reshape(4, 8, 128),
            w_bgate.T.reshape(4, 8, 128),
            w_bproj.T.reshape(4, 8, 128),
            out_gain,
            out_bias,
            w_out,
        )
    ]
    result = pl.pallas_call(
        kernel,
        name="triangle",
        out_shape=pltpu.VMEM((2, 16, 4, 2, 4, 128), BF16),
        in_specs=[any_spec] * 13,
        out_specs=pl.BlockSpec(memory_space=pl.ANY),
        scratch_shapes=[
            pltpu.VMEM((128, 8, 128), BF16),
            pltpu.VMEM((4, 128), jnp.int32),
            pltpu.SMEM((512,), jnp.int32),
            pltpu.SMEM((128,), F32),
            pltpu.SMEM((128,), F32),
            pltpu.SMEM((32,), F32),
            pltpu.SMEM((32,), F32),
                pltpu.VMEM((128, 128), BF16),
            pltpu.VMEM((5, 4, 4, 8, 128), BF16),
            pltpu.VMEM((128, 128), BF16),
            pltpu.VMEM((8, 128), F32),
            pltpu.VMEM((4, 8, 128), F32),
            pltpu.VMEM((1024, 128), F32),
            pltpu.VMEM((1024, 128), F32),
            pltpu.VMEM((1024, 128), F32),
            pltpu.VMEM((1024, 128), F32),
            pltpu.VMEM((8, 16, 8, 128), BF16),
            pltpu.VMEM((4, 8, 4, 8, 128), BF16),
            pltpu.VMEM((8, 16, 8, 128), BF16),
            pltpu.VMEM((16, 16, 8, 128), BF16),
            pltpu.VMEM((2, 8, 16, 4, 128), BF16),
            pltpu.VMEM((2, 128, 4, 128), BF16),
            pltpu.VMEM((2, 8, 16, 4, 128), BF16),
            pltpu.SemaphoreType.DMA((13,)),
            pltpu.SemaphoreType.DMA((10,)),
            pltpu.SemaphoreType.DMA((10,)),
            pltpu.SemaphoreType.DMA((6,)),
            pltpu.SemaphoreType.DMA,
            pltpu.SemaphoreType.DMA((8,)),
            pltpu.SemaphoreType.DMA((8,)),
            pltpu.SemaphoreType.DMA,
            pltpu.SemaphoreType.DMA((4,)),
            pltpu.SemaphoreType.DMA((2,)),
            pltpu.SemaphoreType.DMA((2,)),
            pltpu.SemaphoreType.REGULAR,
        ],
        compiler_params=pltpu.CompilerParams(
            collective_id=0, has_side_effects=True, vmem_limit_bytes=32 << 20
        ),
    )(*operands)
    return result.reshape(32, 32, 128)


def solution(mesh):
    return jax.shard_map(
        on_device,
        mesh=mesh,
        in_specs=(
            P("chan", "row", "col"),
            P(),
            P(),
            P(),
            P(None, "chan"),
            P(None, "chan"),
            P(None, "chan"),
            P(None, "chan"),
            P(None, "chan"),
            P("chan"),
            P("chan"),
            P(),
        ),
        out_specs=P("chan", "row", "col"),
        check_vma=False,
    )
```
